128 devices in a mesh: roll: 32 (over z, x, y_lo), tp: 4 (over y_hi, core).
Axes of the slice: x: 4, y: 4 (y_hi: 2, y_lo: 2; y = y_hi * 2 + y_lo), z: 4, core: 2. Of those that a mesh axis runs over, the one named last changes fastest.
Arguments:
- prompt_states: bfloat16 [4, 8192, 8192], P(None, 'roll'), may hold values from -1500 to 1500
- decode_states: bfloat16 [1024, 8192], P(None, 'roll'), may hold values from -1500 to 1500
- norm_gain: bfloat16 [8192], replicated, may hold values from 0.5 to 1.5
- latent_down: bfloat16 [8192, 2048], P(None, 'tp')
- key_up: bfloat16 [8, 256, 128], P('tp')
- value_up: bfloat16 [8, 256, 128], P('tp'), may hold values from -0.375 to 0.375
- query_weight: bfloat16 [8192, 8192], P('roll', 'tp')
- out_weight: bfloat16 [8192, 8192], P('tp', 'roll'), may hold values from -0.0625 to 0.0625
- prompt_lengths: int32 [4], replicated, may hold values from 4096 to 8192, as said below
- group_prompt: int32 [32], replicated, may hold values from 0 to 3
Outputs:
- attn_out: bfloat16 [1024, 8192], P('tp', 'roll')
The draws below stay inside these ranges and needn't reach their ends.
Inputs may be any that keep to these rules, and one draw needn't show every extreme that they name: `prompt_lengths`: some prompt has all 8192 tokens valid.
All inputs are finite; a program needn't handle non-finite values.
Results may differ from the reference program's by a relative error of at most 0.035.
Values may be sent and summed in bfloat16 or wider, within the bound.
A program may use at most 192 MiB of HBM per device.

```python
import math
import jax
import jax.numpy as jnp
from jax import lax

D = 8192
HEADS = 64
KVG = 8
HD = 128
RANK = 256
PROMPTS = 4
SAMPLES = 8
STEPS = 4
GROUPS = 32
LEN = 8192
ROWS = 1024
QW = 8192


def common_parts(key):
    splits = jax.random.split(key, 6)
    lengths = jax.random.randint(splits[0], (PROMPTS,), LEN // 2, LEN + 1)
    longest = jax.random.randint(splits[1], (), 0, PROMPTS)
    lengths = jnp.where(jnp.arange(PROMPTS) == longest, LEN, lengths).astype(jnp.int32)
    chosen = jax.random.randint(splits[2], (GROUPS,), 0, PROMPTS).astype(jnp.int32)
    column = jnp.exp(jax.random.uniform(splits[3], (D,), jnp.float32, 0.0, math.log(10.0)))
    column = column * 3.0 ** (jnp.arange(D, dtype=jnp.float32) / D)
    down = jax.random.truncated_normal(splits[4], -6.0, 6.0, (D, KVG * RANK), jnp.float32) * D ** (-0.5)
    upward = jax.random.truncated_normal(splits[5], -6.0, 6.0, (KVG, RANK, HD), jnp.float32) * RANK ** (-0.5)
    return (lengths, chosen, column, down, upward)


def entries_of(key, shape):
    splits = jax.random.split(key, 4)
    drawn = jax.random.truncated_normal(splits[0], -4.0, 4.0, shape, jnp.float32)
    values = drawn
    row_shape = shape[:-1] + (1,)
    scales = jnp.exp(jax.random.uniform(splits[3], row_shape, jnp.float32, 0.0, math.log(10.0)))
    return values * scales


def decode_base(key):
    lengths, chosen, column, down, upward = common_parts(key)
    return entries_of(jax.random.fold_in(key, 21), (ROWS, D)) * column


def prompt_base(key):
    lengths, chosen, column, down, upward = common_parts(key)
    values = entries_of(jax.random.fold_in(key, 33), (PROMPTS, LEN, D)) * column
    return values


def draw_prompt_states(key, part):
    values = prompt_base(key)
    return values.astype(jnp.bfloat16)


def draw_decode_states(key, part):
    values = decode_base(key)
    return values.astype(jnp.bfloat16)


def draw_latent_down(key, part):
    lengths, chosen, column, down, upward = common_parts(key)
    return down.astype(jnp.bfloat16)


def draw_key_up(key, part):
    lengths, chosen, column, down, upward = common_parts(key)
    return upward.astype(jnp.bfloat16)


def draw_query_weight(key, part):
    own_key = jax.random.fold_in(key, 5)
    values = jax.random.truncated_normal(own_key, -6.0, 6.0, (D, HEADS * HD), jnp.float32) * D ** (-0.5)
    return values.astype(jnp.bfloat16)


def draw_prompt_lengths(key, part):
    lengths, chosen, column, down, upward = common_parts(key)
    return lengths


def draw_group_prompt(key, part):
    lengths, chosen, column, down, upward = common_parts(key)
    return chosen


def steps_of(rng, dims, shards, smallest, largest):
    gain = 1.0
    for position, blocks in shards:
        steps = jax.random.uniform(jax.random.fold_in(jax.random.fold_in(rng, 6), position), (blocks,), jnp.float32, smallest / len(shards), largest / len(shards))
        gain = gain * jnp.repeat(jnp.exp(steps), dims[position] // blocks).reshape((-1,) + (1,) * (len(dims) - 1 - position))
    return gain


def gaussian(key, extent, scale, reach, cuts=(), kind=jnp.bfloat16):
    array = scale * jax.random.normal(key, extent, jnp.float32)
    if cuts:
        array = array * steps_of(key, extent, cuts, -0.22, 0.18)
    return jnp.clip(array, -reach, reach).astype(kind)


def setup_inputs(seed: int = 0) -> dict:
    keys = jax.random.split(jax.random.key(seed), 11)
    prompt_states = draw_prompt_states(jax.random.fold_in(keys[10], 71), 0)
    decode_states = draw_decode_states(jax.random.fold_in(keys[10], 71), 0)
    norm_gain = jnp.clip(1.0 + 0.1 * jax.random.normal(keys[2], (D,), jnp.float32), 0.5, 1.5).astype(jnp.bfloat16)
    latent_down = draw_latent_down(jax.random.fold_in(keys[10], 71), 0)
    key_up = draw_key_up(jax.random.fold_in(keys[10], 71), 0)
    value_up = gaussian(keys[5], (KVG, RANK, HD), RANK ** -0.5, 0.375, ((0, 4),))
    query_weight = draw_query_weight(jax.random.fold_in(keys[10], 71), 0)
    out_weight = gaussian(keys[7], (QW, D), (HEADS * HD) ** -0.5, 0.0625, ((0, 4), (1, 32)))
    prompt_lengths = draw_prompt_lengths(jax.random.fold_in(keys[10], 71), 0)
    group_prompt = draw_group_prompt(jax.random.fold_in(keys[10], 71), 0)
    return dict(prompt_states=prompt_states, decode_states=decode_states, norm_gain=norm_gain, latent_down=latent_down, key_up=key_up, value_up=value_up, query_weight=query_weight, out_weight=out_weight, prompt_lengths=prompt_lengths, group_prompt=group_prompt)


eps = 1e-06
rope_base = 1000000.0

def rotate(values, positions):
    half_dim = values.shape[-1] // 2
    inverse_freq = rope_base ** (-(jnp.arange(half_dim, dtype=jnp.float32) * 2.0 / values.shape[-1]))
    angles = positions[..., None].astype(jnp.float32) * inverse_freq
    cosine = jnp.cos(angles)
    sines = jnp.sin(angles)
    front_half = values[..., :half_dim]
    back_half = values[..., half_dim:]
    return jnp.concatenate([front_half * cosine - back_half * sines, back_half * cosine + front_half * sines], axis=-1)

def reference(prompt_states, decode_states, norm_gain, latent_down, key_up, value_up, query_weight, out_weight, prompt_lengths, group_prompt):
    per_group = HEADS // KVG
    group_rows = SAMPLES * STEPS
    gain_full = norm_gain.astype(jnp.float32)
    key_wide = key_up.astype(jnp.float32)
    value_wide = value_up.astype(jnp.float32)

    def prefill(states):
        widened = states.astype(jnp.float32)
        inverse_rms = lax.rsqrt(lax.optimization_barrier(jnp.mean(widened * widened, axis=-1, keepdims=True)) + eps)
        normed = (widened * inverse_rms * gain_full).astype(jnp.bfloat16)
        latent = jnp.dot(normed, latent_down, preferred_element_type=jnp.float32).astype(jnp.bfloat16)
        latent = latent.reshape(LEN, KVG, RANK)
        rebuilt = jnp.einsum('nkr,krd->nkd', latent.astype(jnp.float32), key_wide)
        keys_made = rotate(rebuilt, jnp.arange(LEN, dtype=jnp.int32)[:, None]).astype(jnp.bfloat16)
        return (latent, keys_made)
    prompt_latent, prompt_keys = lax.map(prefill, prompt_states)
    widened = decode_states.astype(jnp.float32)
    inverse_rms = lax.rsqrt(lax.optimization_barrier(jnp.mean(widened * widened, axis=-1)) + eps)
    scaled_rows = (widened * gain_full).astype(jnp.bfloat16)
    query_raw = inverse_rms[:, None] * jnp.dot(scaled_rows, query_weight, preferred_element_type=jnp.float32)
    decode_latent = (inverse_rms[:, None] * jnp.dot(scaled_rows, latent_down, preferred_element_type=jnp.float32)).astype(jnp.bfloat16)
    decode_latent = decode_latent.reshape(ROWS, KVG, RANK)
    group_len = prompt_lengths[group_prompt].astype(jnp.int32)
    positions = jnp.repeat(group_len, group_rows) + jnp.arange(ROWS, dtype=jnp.int32) % STEPS
    queries = rotate(query_raw.reshape(ROWS, HEADS, HD), positions[:, None]).astype(jnp.bfloat16)
    rebuilt = jnp.einsum('nkr,krd->nkd', decode_latent.astype(jnp.float32), key_wide)
    decode_keys = rotate(rebuilt, positions[:, None]).astype(jnp.bfloat16)
    row_index = jnp.arange(group_rows, dtype=jnp.int32)
    allowed = (row_index[:, None] // STEPS == row_index[None, :] // STEPS) & (row_index[None, :] <= row_index[:, None])
    scaling = HD ** (-0.5)

    def attend(inputs):
        group_queries, group_keys, group_latent, prompt = inputs
        keys_far = prompt_keys[prompt].astype(jnp.float32)
        latent_far = prompt_latent[prompt].astype(jnp.float32)
        length = prompt_lengths[prompt]
        query_wide = group_queries.astype(jnp.float32).reshape(group_rows, KVG, per_group, HD)
        far_scores = jnp.einsum('rkhd,nkd->rkhn', query_wide, keys_far) * scaling
        far_scores = jnp.where(jnp.arange(LEN, dtype=jnp.int32) < length, far_scores, -jnp.inf)
        self_scores = jnp.einsum('rkhd,nkd->rkhn', query_wide, group_keys.astype(jnp.float32)) * scaling
        self_scores = jnp.where(allowed[:, None, None, :], self_scores, -jnp.inf)
        scores = jnp.concatenate([far_scores, self_scores], axis=-1)
        weights = jax.nn.softmax(scores, axis=-1).astype(jnp.bfloat16).astype(jnp.float32)
        latent_mix = jnp.einsum('rkhn,nkc->rkhc', weights[..., :LEN], latent_far)
        latent_mix = latent_mix + jnp.einsum('rkhn,nkc->rkhc', weights[..., LEN:], group_latent.astype(jnp.float32))
        latent_mix = latent_mix.astype(jnp.bfloat16)
        head_values = jnp.einsum('rkhc,kcd->rkhd', latent_mix.astype(jnp.float32), value_wide).astype(jnp.bfloat16)
        return head_values.reshape(group_rows, HEADS * HD)
    head_out = lax.map(attend, (queries.reshape(GROUPS, group_rows, HEADS, HD), decode_keys.reshape(GROUPS, group_rows, KVG, HD), decode_latent.reshape(GROUPS, group_rows, KVG, RANK), group_prompt))
    head_out = head_out.reshape(ROWS, HEADS * HD)
    return jnp.dot(head_out, out_weight, preferred_element_type=jnp.float32).astype(jnp.bfloat16)
```

```python
import functools

import jax
import jax.numpy as jnp
import numpy as np
from jax import lax
from jax.experimental import pallas as pl
from jax.experimental.pallas import tpu as pltpu
from jax.sharding import PartitionSpec as P

HD = 128
RANK = 256
STEPS = 4
MODEL = 8192
TOKENS = 256
PART = 1280
eps = 1e-06
rope_base = 1000000.0
SCALING = HD ** (-0.5)
NEG = -3.0e38
F32 = jnp.float32
BF16 = jnp.bfloat16
MESH_ID = pl.DeviceIdType.MESH


def rope_tables():
    freq = rope_base ** (-(np.arange(64, dtype=np.float64) * 2.0 / HD))
    freq = np.concatenate([freq, freq])

    def pair(positions):
        angles = positions[:, None] * freq[None, :]
        return np.cos(angles).astype(np.float32), np.sin(angles).astype(np.float32)

    fine = pair(np.arange(TOKENS, dtype=np.float64))
    coarse = pair(np.arange(40, dtype=np.float64) * TOKENS)
    steps = pair(np.arange(32, dtype=np.float64) % STEPS)
    return fine + coarse + steps


def rotate(values, cosine, signed_sine):
    return values * cosine + pltpu.roll(values, 64, 1) * signed_sine


def nt_dot(a, b):
    return lax.dot_general(a, b, (((1,), (1,)), ((), ())), preferred_element_type=F32)


def dot(a, b):
    return jnp.dot(a, b, preferred_element_type=F32)


def merge(outs, maxes, sums):
    top = functools.reduce(jnp.maximum, maxes)
    factors = [jnp.exp(m - top) for m in maxes]
    total = sum(f * s for f, s in zip(factors, sums))
    mixed = sum(f * o for f, o in zip(factors, outs))
    return mixed, top, total


def kernel(
    x_ref, gain_ref, wq_ref, ku_ref, vu_ref, wo_ref,
    c0_ref, s0_ref, c1_ref, s1_ref, ct_ref, st_ref,
    len_ref, gp_ref, down_hbm, ps_hbm,
    out_ref,
    slab, wd, xb, acc, sqacc, pp, r1, r2, p2, r3, p3, r4, sq, sqr,
    kb, vb, vut, qq, oo, orr, stt, sttr, o2, o2r, st2, st2r, selfo, selfs, hh, wor, ob, obr,
    loc_sem, q1s, q1r, q2s, q2r, q3s, q3r, sqs, sqrs, kvs, kvr,
    a1s, a1r, a2s, a2r, b1s, b1r, b2s, b2r, b3s, b3r, h1s, h1r, h2s, h2r, wos, worr, obs, obrr,
):
    roll = lax.axis_index("roll")
    t = lax.axis_index("tp")
    z, x, y = roll // 8, (roll // 2) % 4, roll % 2
    coord = ((z, x), (x, z))

    def dev(zz, xx, yy, tt):
        return {"roll": zz * 8 + xx * 2 + yy, "tp": tt}

    def first_dev(part, f):
        return dev(f, x, y, t) if part == 0 else dev(z, f, y, t)

    def second_dev(part, s):
        return dev(z, s, y, t) if part == 0 else dev(s, x, y, t)

    y_dev = dev(z, x, 1 - y, t)

    def remote(src, dst, ss, rs, where):
        return pltpu.make_async_remote_copy(
            src_ref=src, dst_ref=dst, send_sem=ss, recv_sem=rs, device_id=where, device_id_type=MESH_ID
        )

    def landed(dst, ss, rs):
        remote(dst, dst, ss, rs, y_dev).wait_recv()

    def sent(src, ss, rs):
        remote(src, src, ss, rs, y_dev).wait_send()

    def other(i, k):
        return (i + k) % 4

    slab_copy = pltpu.make_async_copy(
        down_hbm.at[pl.ds(pl.multiple_of(roll * 256, 256), 256)], slab, loc_sem.at[0]
    )
    slab_copy.start()
    down_copy = pltpu.make_async_copy(down_hbm, wd, loc_sem.at[1])
    down_copy.start()

    def load_prompt(p):
        return pltpu.make_async_copy(ps_hbm.at[p], xb.at[p % 2], loc_sem.at[2 + p])

    load_prompt(0).start()
    load_prompt(1).start()

    barrier = pltpu.get_barrier_semaphore()
    peers = [dev(other(z, k), x, y, t) for k in (1, 2, 3)]
    peers += [dev(z, other(x, k), y, t) for k in (1, 2, 3)]
    peers += [dev(z, x, y, other(t, k)) for k in (1, 2, 3)]
    peers += [dev(z, x, 1 - y, other(t, k)) for k in (0, 1, 2, 3)]
    for peer in peers:
        pl.semaphore_signal(barrier, inc=1, device_id=peer, device_id_type=MESH_ID)

    gain_slab = gain_ref[:, pl.ds(pl.multiple_of(roll * 256, 256), 256)].astype(F32)
    slab_copy.wait()

    def project(part, d):
        rows = x_ref[d] if part == 0 else x_ref[:, d]
        rows = (rows.reshape(256, 256).astype(F32) * gain_slab).astype(BF16)
        for c in range(4):
            got = dot(rows, wq_ref[:, part * 1024 + c * 256 : part * 1024 + (c + 1) * 256])
            pp[part, d, :, :, c * 256 : (c + 1) * 256] = got.astype(BF16).reshape(4, 64, 256)
        got = dot(rows, slab[:, part * 256 : (part + 1) * 256])
        pp[part, d, :, :, 1024:1280] = got.astype(BF16).reshape(4, 64, 256)

    def q1(part, k):
        m = coord[part][0]
        right, left = first_dev(part, other(m, 1)), first_dev(part, other(m, 3))
        lo, hi = pl.ds(0, 2), pl.ds(2, 2)
        far, near_r, near_l = other(m, 2), other(m, 1), other(m, 3)
        src, dst, where = (
            (pp.at[part, far, lo], r1.at[part, 0], right),
            (pp.at[part, far, hi], r1.at[part, 1], left),
            (pp.at[part, near_r, hi], r2.at[part, 0, hi], right),
            (pp.at[part, near_l, lo], r2.at[part, 1, lo], left),
            (pp.at[part, near_r, lo], r2.at[part, 0, lo], right),
            (pp.at[part, near_l, hi], r2.at[part, 1, hi], left),
        )[k]
        return remote(src, dst, q1s.at[part, k], q1r.at[part, k], where)

    for part in (0, 1):
        project(part, other(coord[part][0], 2))
    pl.semaphore_wait(barrier, len(peers))
    for part in (0, 1):
        q1(part, 0).start()
        q1(part, 1).start()
    for part in (0, 1):
        project(part, other(coord[part][0], 1))
        q1(part, 2).start()
    for part in (0, 1):
        project(part, other(coord[part][0], 3))
        q1(part, 3).start()
    for part in (0, 1):
        project(part, coord[part][0])

    ones = jnp.ones((8, 256), BF16)
    sub8 = lax.broadcasted_iota(jnp.int32, (8, 128), 0)
    squares = jnp.zeros((8, 128), F32)
    for i in range(8):
        rows = x_ref[i // 2, (i % 2) * 2 : (i % 2) * 2 + 2].reshape(128, 256).astype(F32)
        rows = rows * rows
        high = rows.astype(BF16)
        low = (rows - high.astype(F32)).astype(BF16)
        squares = jnp.where(sub8 == i, nt_dot(ones, high) + nt_dot(ones, low), squares)
    sq[0] = squares

    def square_copies(stage):
        if stage == 2:
            return [remote(sq.at[2], sqr.at[2, y], sqs.at[2, 1], sqrs.at[2, y], y_dev)]
        me = (z, x)[stage]
        return [
            remote(
                sq.at[stage], sqr.at[stage, me], sqs.at[stage, k], sqrs.at[stage, me],
                (dev(other(me, k), x, y, t), dev(z, other(me, k), y, t))[stage],
            )
            for k in (1, 2, 3)
        ]

    def square_sum(stage):
        total = sq[stage]
        others = [other((z, x)[stage], k) for k in (1, 2, 3)] if stage < 2 else [1 - y]
        for o in others:
            landed(sqr.at[stage, o], sqs.at[stage, 1], sqrs.at[stage, o])
            total = total + sqr[stage, o]
        return total

    for c in square_copies(0):
        c.start()

    sign = jnp.where(lax.broadcasted_iota(jnp.int32, (1, HD), 1) < 64, -1.0, 1.0)
    far_c, far_s = c1_ref[pl.ds(roll, 1), :], s1_ref[pl.ds(roll, 1), :]
    for k in (0, 1):
        vut[k] = jnp.transpose(vu_ref[k].astype(F32)).astype(BF16)

    def kv_copies(p):
        return [
            remote(b.at[y, p], b.at[y, p], kvs.at[i, p], kvr.at[i, p], y_dev)
            for i, b in enumerate((kb, vb))
        ]

    def prompt_block(p):
        load_prompt(p).wait()
        if p == 0:
            down_copy.wait()
        acc[...] = jnp.zeros_like(acc)
        sqacc[...] = jnp.zeros_like(sqacc)

        def step(i, carry):
            cols = pl.ds(pl.multiple_of(i * 1024, 1024), 1024)
            wide = xb[p % 2, :, cols].astype(F32)
            sq_wide = wide * wide
            part_sq = sq_wide[:, 0:128]
            for j in range(1, 8):
                part_sq = part_sq + sq_wide[:, j * 128 : (j + 1) * 128]
            sqacc[...] += part_sq
            scaled = (wide * gain_ref[:, cols].astype(F32)).astype(BF16)
            acc[...] += dot(scaled, wd[cols, :])
            return carry

        lax.fori_loop(0, 8, step, 0)
        if p < 2:
            load_prompt(p + 2).start()
        inverse = lax.rsqrt(jnp.sum(sqacc[...], axis=1, keepdims=True) / MODEL + eps)
        latent = (acc[...] * inverse).astype(BF16)
        cosine = far_c * c0_ref[...] - far_s * s0_ref[...]
        sine = (far_s * c0_ref[...] + far_c * s0_ref[...]) * sign
        for k in (0, 1):
            mine = latent[:, k * RANK : (k + 1) * RANK]
            kb[y, p, k] = rotate(dot(mine, ku_ref[k]), cosine, sine).astype(BF16)
            vb[y, p, k] = nt_dot(vut[k], mine).astype(BF16)
        for c in kv_copies(p):
            c.start()

    prompt_block(0)
    prompt_block(1)

    def add_into(dst, sources, blocks):
        def step(i, carry):
            rows = pl.ds(pl.multiple_of((i % 2) * 32, 32), 32)
            total = sources[0][i // 2, rows, :].astype(F32)
            for source in sources[1:]:
                total = total + source[i // 2, rows, :].astype(F32)
            dst[i // 2, rows, :] = total.astype(BF16)
            return carry

        lax.fori_loop(0, 2 * blocks, step, 0)

    for part in (0, 1):
        m = coord[part][0]
        for k, d, half in ((0, other(m, 1), 0), (1, other(m, 3), 2)):
            landed(r1.at[part, k], q1s.at[part, k], q1r.at[part, k])
            spot = pp.at[part, d, pl.ds(half, 2)]
            add_into(spot, (spot, r1.at[part, k]), 2)
            q1(part, 4 + k).start()
    sq[1] = square_sum(0)
    for c in square_copies(1):
        c.start()

    prompt_block(2)
    prompt_block(3)

    def q2(part, k):
        n = coord[part][1]
        s = other(n, k)
        return remote(p2.at[part, s], r3.at[part, n], q2s.at[part, k], q2r.at[part, n], second_dev(part, s))

    for part in (0, 1):
        m = coord[part][0]
        for k, d, half in ((2, 0, 2), (3, 1, 0), (4, 0, 0), (5, 1, 2)):
            landed(r2.at[part, d, pl.ds(half, 2)], q1s.at[part, k], q1r.at[part, k])
        add_into(p2.at[part], (pp.at[part, m], r2.at[part, 0], r2.at[part, 1]), 4)
        for k in (2, 1, 3):
            q2(part, k).start()
    sq[2] = square_sum(1)
    for c in square_copies(2):
        c.start()

    def q3(part):
        src = p3.at[part, pl.ds(pl.multiple_of((1 - y) * 32, 32), 32)]
        return remote(src, r4.at[part], q3s.at[part], q3r.at[part], y_dev)

    for part in (0, 1):
        n = coord[part][1]
        for k in (1, 3, 2):
            o = other(n, k)
            landed(r3.at[part, o], q2s.at[part, k], q2r.at[part, o])
        total = p2[part, n].astype(F32)
        for k in (1, 2, 3):
            total = total + r3[part, other(n, k)].astype(F32)
        p3[part] = total.astype(BF16)
        q3(part).start()

    prompt = gp_ref[roll]
    length = len_ref[prompt]
    hi_c, hi_s = c1_ref[pl.ds(length >> 8, 1), :], s1_ref[pl.ds(length >> 8, 1), :]
    lo_c, lo_s = c0_ref[pl.ds(length & 255, 1), :], s0_ref[pl.ds(length & 255, 1), :]
    len_c, len_s = hi_c * lo_c - hi_s * lo_s, hi_s * lo_c + hi_c * lo_s
    row_c = len_c * ct_ref[...] - len_s * st_ref[...]
    row_s = (len_s * ct_ref[...] + len_c * st_ref[...]) * sign
    all_squares = square_sum(2)
    row_squares = jnp.sum(jnp.where(sub8 == roll // 4, all_squares, 0.0), axis=0, keepdims=True)
    lane = lax.broadcasted_iota(jnp.int32, (32, 128), 1)
    sub = lax.broadcasted_iota(jnp.int32, (32, 128), 0)
    row_squares = jnp.sum(
        jnp.where(lane == (roll % 4) * 32 + sub, row_squares, 0.0), axis=1, keepdims=True
    )
    inverse = lax.rsqrt(row_squares / MODEL + eps)

    def a1(part, k):
        m, n = coord[part]
        f = other(m, k)
        return remote(qq.at[part, m, n], qq.at[part, m, n], a1s.at[part, k], a1r.at[part, m], first_dev(part, f))

    def a2(part, f, k):
        n = coord[part][1]
        return remote(
            qq.at[part, f, n], qq.at[part, f, n], a2s.at[part, f, k], a2r.at[part, f, n],
            second_dev(part, other(n, k)),
        )

    kept = []
    for part in (0, 1):
        m, n = coord[part]
        landed(r4.at[part], q3s.at[part], q3r.at[part])
        own = p3[part, pl.ds(pl.multiple_of(y * 32, 32), 32), :].astype(F32) + r4[part].astype(F32)
        own = own * inverse
        heads = [rotate(own[:, h * HD : (h + 1) * HD], row_c, row_s) for h in range(8)]
        queries = jnp.transpose(jnp.concatenate(heads, axis=0)).astype(BF16)
        qq[part, m, n] = queries
        for k in (2, 1, 3):
            a1(part, k).start()
        for k in (2, 1, 3):
            a2(part, m, k).start()
        kept.append((queries, own[:, 1024:1280].astype(BF16)))

    wo_copy = remote(wo_ref, wor, wos, worr, y_dev)
    wo_copy.start()

    key_i = lax.broadcasted_iota(jnp.int32, (32, 256), 0)
    row_i = lax.broadcasted_iota(jnp.int32, (32, 256), 1) % 32
    allowed = (key_i // STEPS == row_i // STEPS) & (key_i <= row_i)
    for part in (0, 1):
        queries, latent = kept[part]
        keys = rotate(dot(latent, ku_ref[part]), row_c, row_s).astype(BF16)
        scores = jnp.where(allowed, dot(keys, queries) * SCALING, NEG)
        top = jnp.max(scores, axis=0, keepdims=True)
        weights = jnp.exp(scores - top)
        values = nt_dot(vut[part], latent).astype(BF16)
        selfo[part] = dot(values, weights.astype(BF16))
        selfs[part, 0:1, :] = top
        selfs[part, 1:2, :] = jnp.sum(weights, axis=0, keepdims=True)

    for p in range(4):
        for i, b in enumerate((kb, vb)):
            landed(b.at[1 - y, p], kvs.at[i, p], kvr.at[i, p])
    base = (z * 4 + x) * (2 * TOKENS)
    token = lax.broadcasted_iota(jnp.int32, (TOKENS, 256), 0)

    def attend(part, f, s):
        group = (f * 8 + s * 2 if part == 0 else s * 8 + f * 2) + y
        chosen = gp_ref[group]
        limit = len_ref[chosen] - base
        queries = qq[part, f, s]
        scores = []
        for half in (0, 1):
            raw = dot(kb[half, chosen, part], queries) * SCALING
            scores.append(jnp.where(token < limit - half * TOKENS, raw, NEG))
        top = jnp.max(jnp.maximum(scores[0], scores[1]), axis=0, keepdims=True)
        weights = [jnp.exp(sc - top) for sc in scores]
        total = jnp.sum(weights[0] + weights[1], axis=0, keepdims=True)
        mixed = dot(vb[0, chosen, part], weights[0].astype(BF16))
        mixed = mixed + dot(vb[1, chosen, part], weights[1].astype(BF16))
        oo[part, f, s] = mixed.astype(BF16)
        stt[part, s, f, 0:1, :] = top
        stt[part, s, f, 1:2, :] = total

    def b1(part, f, s):
        n = coord[part][1]
        return remote(
            oo.at[part, f, s], orr.at[part, n, f], b1s.at[part, f, s], b1r.at[part, n, f], second_dev(part, s)
        )

    def b2(part, s):
        n = coord[part][1]
        return remote(stt.at[part, s], sttr.at[part, n], b2s.at[part, s], b2r.at[part, n], second_dev(part, s))

    for part in (0, 1):
        m, n = coord[part]
        for k in (1, 3, 2):
            f = other(m, k)
            landed(qq.at[part, f, n], a1s.at[part, k], a1r.at[part, f])
            for j in (2, 1, 3):
                a2(part, f, j).start()

    def own_column(i, carry):
        for part in (0, 1):
            m, n = coord[part]
            attend(part, other(m, i), n)
        return carry

    lax.fori_loop(0, 4, own_column, 0)

    def far_column(i, carry):
        for part in (0, 1):
            m, n = coord[part]
            f, s = other(m, i // 3), other(n, 1 + i % 3)
            landed(qq.at[part, f, s], a2s.at[part, 0, 0], a2r.at[part, f, s])
            attend(part, f, s)
            b1(part, f, s).start()
        return carry

    lax.fori_loop(0, 12, far_column, 0)
    for part in (0, 1):
        for k in (1, 2, 3):
            b2(part, other(coord[part][1], k)).start()

    def b3(part, f):
        m = coord[part][0]
        return (
            remote(o2.at[part, f], o2r.at[part, m], b3s.at[0, part, f], b3r.at[0, part, m], first_dev(part, f)),
            remote(st2.at[part, f], st2r.at[part, m], b3s.at[1, part, f], b3r.at[1, part, m], first_dev(part, f)),
        )

    for part in (0, 1):
        n = coord[part][1]
        for k in (1, 2, 3):
            o = other(n, k)
            landed(sttr.at[part, o], b2s.at[part, 0], b2r.at[part, o])

    def merge_column(part, f):
        n = coord[part][1]
        outs, maxes, sums = [oo[part, f, n].astype(F32)], [stt[part, n, f, 0:1, :]], [stt[part, n, f, 1:2, :]]
        for k in (1, 2, 3):
            o = other(n, k)
            landed(orr.at[part, o, f], b1s.at[part, 0, 0], b1r.at[part, o, f])
            outs.append(orr[part, o, f].astype(F32))
            maxes.append(sttr[part, o, f, 0:1, :])
            sums.append(sttr[part, o, f, 1:2, :])
        mixed, top, total = merge(outs, maxes, sums)
        o2[part, f] = mixed.astype(BF16)
        st2[part, f, 0:1, :] = top
        st2[part, f, 1:2, :] = total

    def merge_far(i, carry):
        for part in (0, 1):
            f = other(coord[part][0], i)
            merge_column(part, f)
            for c in b3(part, f):
                c.start()
        return carry

    lax.fori_loop(1, 4, merge_far, 0)
    for part in (0, 1):
        merge_column(part, coord[part][0])

    def h1(part, k):
        m, n = coord[part]
        return remote(
            hh.at[part, m, n], hh.at[part, m, n], h1s.at[part, k], h1r.at[part, m], first_dev(part, other(m, k))
        )

    def h2(part, f, k):
        n = coord[part][1]
        return remote(
            hh.at[part, f, n], hh.at[part, f, n], h2s.at[part, f, k], h2r.at[part, f, n],
            second_dev(part, other(n, k)),
        )

    for part in (0, 1):
        m, n = coord[part]
        outs = [selfo[part], o2[part, m].astype(F32)]
        maxes = [selfs[part, 0:1, :], st2[part, m, 0:1, :]]
        sums = [selfs[part, 1:2, :], st2[part, m, 1:2, :]]
        for k in (1, 3, 2):
            f = other(m, k)
            landed(o2r.at[part, f], b3s.at[0, part, 0], b3r.at[0, part, f])
            landed(st2r.at[part, f], b3s.at[1, part, 0], b3r.at[1, part, f])
            outs.append(o2r[part, f].astype(F32))
            maxes.append(st2r[part, f, 0:1, :])
            sums.append(st2r[part, f, 1:2, :])
        mixed, _, total = merge(outs, maxes, sums)
        heads = jnp.transpose(mixed / total).astype(BF16)
        for h in range(8):
            hh[part, m, n, :, h * HD : (h + 1) * HD] = heads[h * 32 : (h + 1) * 32, :]
        for k in (2, 1, 3):
            h1(part, k).start()
        for k in (2, 1, 3):
            h2(part, m, k).start()
    for part in (0, 1):
        m, n = coord[part]
        for k in (1, 3, 2):
            f = other(m, k)
            landed(hh.at[part, f, n], h1s.at[part, k], h1r.at[part, f])
            for j in (2, 1, 3):
                h2(part, f, j).start()
    wo_copy.wait_recv()
    for part in (0, 1):
        m, n = coord[part]
        for i in range(4):
            f = other(m, i)
            for k in (1, 3, 2):
                s = other(n, k)
                landed(hh.at[part, f, s], h2s.at[part, 0, 1], h2r.at[part, f, s])

    def out_block(tt):
        left = hh[0, tt].reshape(128, 1024)
        right = hh[1, :, tt].reshape(128, 1024)
        for where, weight in ((y, wo_ref), (1 - y, wor)):
            got = dot(left, weight[0:1024, :]) + dot(right, weight[1024:2048, :])
            ob[tt, where] = got.astype(BF16)

    def out_copy(tt, yy):
        return remote(ob.at[tt, yy], obr.at[t, y], obs.at[tt, yy], obrr.at[t, y], dev(z, x, yy, tt))

    for k in (2, 1, 3, 0):
        tt = other(t, k)
        out_block(tt)
        out_copy(tt, 1 - y).start()
        if k:
            out_copy(tt, y).start()
    for yy_k in (0, 1):
        yy = y if yy_k == 0 else 1 - y
        total = ob[t, y].astype(F32) if yy_k == 0 else None
        for k in ((1, 3, 2) if yy_k == 0 else (0, 1, 3, 2)):
            tt = other(t, k)
            landed(obr.at[tt, yy], obs.at[0, 0], obrr.at[tt, yy])
            piece = obr[tt, yy].astype(F32)
            total = piece if total is None else total + piece
        out_ref[:, yy] = total.astype(BF16).reshape(4, 32, 256)

    for part in (0, 1):
        m, n = coord[part]
        for k in range(6):
            q1(part, k).wait_send()
        for k in (1, 2, 3):
            q2(part, k).wait_send()
            a1(part, k).wait_send()
            h1(part, k).wait_send()
            b2(part, other(n, k)).wait_send()
            for c in b3(part, other(m, k)):
                c.wait_send()
        q3(part).wait_send()
        for i in range(4):
            for k in (1, 2, 3):
                a2(part, other(m, i), k).wait_send()
                h2(part, other(m, i), k).wait_send()
                b1(part, other(m, i), other(n, k)).wait_send()
    for stage in range(3):
        for c in square_copies(stage):
            c.wait_send()
    for p in range(4):
        for c in kv_copies(p):
            c.wait_send()
    wo_copy.wait_send()
    for k in (0, 1, 2, 3):
        out_copy(other(t, k), 1 - y).wait_send()
        if k:
            out_copy(other(t, k), y).wait_send()


def local(
    prompt_states, decode_states, norm_gain, latent_down, key_up, value_up, query_weight, out_weight,
    prompt_lengths, group_prompt,
):
    tables = [jnp.asarray(v) for v in rope_tables()]
    vmem = pl.BlockSpec(memory_space=pltpu.VMEM)
    smem = pl.BlockSpec(memory_space=pltpu.SMEM)
    hbm = pl.BlockSpec(memory_space=pl.ANY)
    V, D = pltpu.VMEM, pltpu.SemaphoreType.DMA
    scratch = [
        V((256, 512), BF16), V((MODEL, 512), BF16), V((2, TOKENS, MODEL), BF16),
        V((TOKENS, 512), F32), V((TOKENS, 128), F32),
        V((2, 4, 4, 64, PART), BF16), V((2, 2, 2, 64, PART), BF16), V((2, 2, 4, 64, PART), BF16),
        V((2, 4, 64, PART), BF16), V((2, 4, 64, PART), BF16), V((2, 64, PART), BF16), V((2, 32, PART), BF16),
        V((3, 8, 128), F32), V((3, 4, 8, 128), F32),
        V((2, 4, 2, TOKENS, HD), BF16), V((2, 4, 2, HD, TOKENS), BF16), V((2, HD, RANK), BF16),
        V((2, 4, 4, HD, 256), BF16), V((2, 4, 4, HD, 256), BF16), V((2, 4, 4, HD, 256), BF16),
        V((2, 4, 4, 8, 256), F32), V((2, 4, 4, 8, 256), F32),
        V((2, 4, HD, 256), BF16), V((2, 4, HD, 256), BF16), V((2, 4, 8, 256), F32), V((2, 4, 8, 256), F32),
        V((2, HD, 256), F32), V((2, 8, 256), F32),
        V((2, 4, 4, 32, 1024), BF16), V((2048, 256), BF16),
        V((4, 2, 128, 256), BF16), V((4, 2, 128, 256), BF16),
        D((6,)), D((2, 6)), D((2, 6)), D((2, 4)), D((2, 4)), D((2,)), D((2,)), D((3, 4)), D((3, 4)),
        D((2, 4)), D((2, 4)),
        D((2, 4)), D((2, 4)), D((2, 4, 4)), D((2, 4, 4)), D((2, 4, 4)), D((2, 4, 4)), D((2, 4)), D((2, 4)),
        D((2, 2, 4)), D((2, 2, 4)), D((2, 4)), D((2, 4)), D((2, 4, 4)), D((2, 4, 4)), D, D,
        D((4, 2)), D((4, 2)),
    ]
    out = pl.pallas_call(
        kernel,
        out_shape=jax.ShapeDtypeStruct((4, 2, 32, 256), BF16),
        in_specs=[vmem] * 12 + [smem] * 2 + [hbm] * 2,
        out_specs=vmem,
        scratch_shapes=scratch,
        compiler_params=pltpu.CompilerParams(
            collective_id=0, has_side_effects=True, vmem_limit_bytes=60 * 1024 * 1024
        ),
        cost_estimate=pl.CostEstimate(flops=16_000_000_000, bytes_accessed=30_000_000, transcendentals=5_000_000),
        name="decode_attention",
    )(
        decode_states.reshape(4, 4, 64, 256), norm_gain.reshape(1, MODEL), query_weight, key_up, value_up,
        out_weight, *tables, prompt_lengths, group_prompt, latent_down, prompt_states,
    )
    return out.reshape(256, 256)


def solution(mesh):
    return jax.shard_map(
        local,
        mesh=mesh,
        in_specs=(
            P(None, "roll", None),
            P(None, "roll"),
            P(),
            P(None, "tp"),
            P("tp", None, None),
            P("tp", None, None),
            P("roll", "tp"),
            P("tp", "roll"),
            P(),
            P(),
        ),
        out_specs=P("tp", "roll"),
        check_vma=False,
    )
```

```python
import functools

import jax
import jax.numpy as jnp
import numpy as np
from jax import lax
from jax.experimental import pallas as pl
from jax.experimental.pallas import tpu as pltpu
from jax.sharding import PartitionSpec as P

HD = 128
RANK = 256
STEPS = 4
MODEL = 8192
TOKENS = 256
NEAR = 1024
PAIR = 256
MIX = HD + 16
eps = 1e-06
rope_base = 1000000.0
SCALE2 = HD ** (-0.5) * float(np.log2(np.e))
NEG = -1.0e38
F32 = jnp.float32
BF16 = jnp.bfloat16
MESH_ID = pl.DeviceIdType.MESH


def rope_tables():
    freq = rope_base ** (-(np.arange(64, dtype=np.float64) * 2.0 / HD))
    freq = np.concatenate([freq, freq])

    def pair(positions):
        angles = positions[:, None] * freq[None, :]
        return np.cos(angles).astype(np.float32), np.sin(angles).astype(np.float32)

    fine = pair(np.arange(TOKENS, dtype=np.float64))
    coarse = pair(np.arange(40, dtype=np.float64) * TOKENS)
    steps = pair(np.arange(32, dtype=np.float64) % STEPS)
    return fine + coarse + steps


def rotate(values, cosine, signed_sine):
    return values * cosine + pltpu.roll(values, 64, 1) * signed_sine


def nt_dot(a, b):
    return lax.dot_general(a, b, (((1,), (1,)), ((), ())), preferred_element_type=F32)


def dot(a, b):
    return jnp.dot(a, b, preferred_element_type=F32)


def merge(outs, maxes, sums):
    top = functools.reduce(jnp.maximum, maxes)
    factors = [jnp.exp2(m - top) for m in maxes]
    total = sum(f * s for f, s in zip(factors, sums))
    mixed = sum(f * o for f, o in zip(factors, outs))
    return mixed, top, total


def terms(value):
    high = value.astype(BF16).astype(F32)
    rest = value - high
    middle = rest.astype(BF16).astype(F32)
    return [high, middle, rest - middle]


def store(ref, mixed, top, total):
    ref[0:HD] = mixed.astype(BF16)
    row = lax.broadcasted_iota(jnp.int32, (16, top.shape[1]), 0)
    tail = jnp.zeros((16, top.shape[1]), F32)
    for i, term in enumerate(terms(top) + terms(total)):
        tail = jnp.where(row == i, term, tail)
    ref[HD:MIX] = tail.astype(BF16)


def fetch(ref):
    tail = ref[HD:MIX].astype(F32)
    top = tail[0:1] + tail[1:2] + tail[2:3]
    total = tail[3:4] + tail[4:5] + tail[5:6]
    return ref[0:HD].astype(F32), top, total


def kernel(
    x_ref, gain_ref, ku_ref, vu_ref,
    c0_ref, s0_ref, c1_ref, s1_ref, ct_ref, st_ref,
    len_ref, gp_ref, wq_hbm, down_hbm, wo_hbm, ps_hbm,
    out_ref,
    gain_row, slab, wo_ref, wd, xb, acc, sqacc, xs, xo, xn, xns, wq,
    pn, pg, r1n, r1g, r2n, r2g, p2n, p2g, r3n, r3g, p3, r4, sq, sqr,
    kb, vb, vut, bias, qq, oo, orr, o2, o2r, selfo, selfs, hh, wor, ob, obc, ob2, obr,
    loc_sem, wq_sem, xws, xwr, q1s, q1r, q2s, q2r, q3s, q3r, sqs, sqrs, kvs, kvr,
    a1s, a1r, a2s, a2r, b1s, b1r, b3s, b3r, h1r, h2r, wos, worr,
    ocs, ocr, obs, obrr,
):
    roll = lax.axis_index("roll")
    t = lax.axis_index("tp")
    z, x, y = roll // 8, (roll // 2) % 4, roll % 2
    coord = ((z, x), (x, z))

    def dev(zz, xx, yy, tt):
        return {"roll": zz * 8 + xx * 2 + yy, "tp": tt}

    def first_dev(part, f):
        return dev(f, x, y, t) if part == 0 else dev(z, f, y, t)

    def second_dev(part, s):
        return dev(z, s, y, t) if part == 0 else dev(s, x, y, t)

    y_dev = dev(z, x, 1 - y, t)
    core = t % 2
    core_dev = dev(z, x, y, t + 1 - 2 * core)

    def remote(src, dst, ss, rs, where):
        return pltpu.make_async_remote_copy(
            src_ref=src, dst_ref=dst, send_sem=ss, recv_sem=rs, device_id=where, device_id_type=MESH_ID
        )

    def landed(dst, ss, rs):
        remote(dst, dst, ss, rs, y_dev).wait_recv()

    def sent(src, ss, rs):
        remote(src, src, ss, rs, y_dev).wait_send()

    def other(i, k):
        return (i + k) % 4

    slab_copy = pltpu.make_async_copy(
        down_hbm.at[pl.ds(pl.multiple_of((roll - y) * 256, 256), 512)], slab, loc_sem.at[0]
    )
    slab_copy.start()
    wq_copies = [
        pltpu.make_async_copy(wq_hbm.at[:, i * NEAR : (i + 1) * NEAR], wq.at[i], wq_sem.at[i]) for i in range(2)
    ]
    for c in wq_copies:
        c.start()
    down_copy = pltpu.make_async_copy(down_hbm, wd, loc_sem.at[1])
    down_copy.start()

    def load_prompt(p):
        return pltpu.make_async_copy(ps_hbm.at[p], xb.at[p % 2], loc_sem.at[2 + p])

    load_prompt(0).start()
    load_prompt(1).start()
    wo_load = pltpu.make_async_copy(wo_hbm, wo_ref, loc_sem.at[6])
    wo_load.start()

    barrier = pltpu.get_barrier_semaphore()
    peers = [dev(other(z, k), x, y, t) for k in (1, 2, 3)]
    peers += [dev(z, other(x, k), y, t) for k in (1, 2, 3)]
    peers += [y_dev, core_dev, dev(z, x, y, (t + 2) % 4), dev(z, x, 1 - y, (t + 2) % 4)]
    for peer in peers:
        pl.semaphore_signal(barrier, inc=1, device_id=peer, device_id_type=MESH_ID)

    streams = ((pn, r1n, r2n, p2n, r3n), (pg, r1g, r2g, p2g, r3g))

    def gain_of(owner):
        return gain_row[:, pl.ds(pl.multiple_of(owner * 256, 256), 256)]

    for i in range(8):
        gain_row[:, i * 1024 : (i + 1) * 1024] = gain_ref[i * 1024 : (i + 1) * 1024].astype(F32).reshape(1, 1024)
    own_gain = gain_of(roll)
    xo[...] = x_ref[:, :, 1 - y]
    for c in wq_copies:
        c.wait()
    for d in range(4):
        rows = x_ref[d].reshape(256, 256).astype(F32) * own_gain
        xs[d] = rows.astype(BF16).reshape(4, 2, 32, 256)

    def project_near(part, d):
        rows = (xs[d] if part == 0 else xs[:, d]).reshape(256, 256)
        for c in range(4):
            got = dot(rows, wq[part, :, c * 256 : (c + 1) * 256])
            pn[part, d, :, :, c * 256 : (c + 1) * 256] = got.astype(BF16).reshape(4, 64, 256)

    def project_pair(part, d):
        mine = (xs[d, :, y] if part == 0 else xs[:, d, y]).reshape(128, 256)
        theirs = (xns[d] if part == 0 else xns[:, d]).reshape(128, 256)
        cols = slice(part * RANK, (part + 1) * RANK)
        got = dot(mine, slab[pl.ds(pl.multiple_of(y * 256, 256), 256), cols])
        got = got + dot(theirs, slab[pl.ds(pl.multiple_of((1 - y) * 256, 256), 256), cols])
        pg[part, d] = got.astype(BF16).reshape(4, 32, 256)

    def q1(stream, part, k):
        pp, r1, r2 = streams[stream][:3]
        m = coord[part][0]
        right, left = first_dev(part, other(m, 1)), first_dev(part, other(m, 3))
        lo, hi = pl.ds(0, 2), pl.ds(2, 2)
        far, near_r, near_l = other(m, 2), other(m, 1), other(m, 3)
        src, dst, where = (
            (pp.at[part, far, lo], r1.at[part, 0], right),
            (pp.at[part, far, hi], r1.at[part, 1], left),
            (pp.at[part, near_r, hi], r2.at[part, 0, hi], right),
            (pp.at[part, near_l, lo], r2.at[part, 1, lo], left),
            (pp.at[part, near_r, lo], r2.at[part, 0, lo], right),
            (pp.at[part, near_l, hi], r2.at[part, 1, hi], left),
        )[k]
        return remote(src, dst, q1s.at[stream, part, k], q1r.at[stream, part, k], where)

    def add_into(dst, sources, blocks, per):
        def step(i, carry):
            rows = pl.ds(pl.multiple_of((i % per) * 32, 32), 32)
            total = sources[0][i // per, rows, :].astype(F32)
            for source in sources[1:]:
                total = total + source[i // per, rows, :].astype(F32)
            dst[i // per, rows, :] = total.astype(BF16)
            return carry

        lax.fori_loop(0, per * blocks, step, 0)

    def q1_forward(stream, part):
        pp, r1 = streams[stream][:2]
        m = coord[part][0]
        for k, d, half in ((0, other(m, 1), 0), (1, other(m, 3), 2)):
            landed(r1.at[part, k], q1s.at[stream, part, k], q1r.at[stream, part, k])
            spot = pp.at[part, d, pl.ds(half, 2)]
            add_into(spot, (spot, r1.at[part, k]), 2, 2 - stream)
            q1(stream, part, 4 + k).start()

    def q2(stream, part, k):
        p2, r3 = streams[stream][3:]
        n = coord[part][1]
        s = other(n, k)
        return remote(
            p2.at[part, s], r3.at[part, n], q2s.at[stream, part, k], q2r.at[stream, part, n], second_dev(part, s)
        )

    def q1_finish(stream, part):
        pp, _, r2, p2, _ = streams[stream]
        m = coord[part][0]
        for k, d, half in ((2, 0, 2), (3, 1, 0), (4, 0, 0), (5, 1, 2)):
            landed(r2.at[part, d, pl.ds(half, 2)], q1s.at[stream, part, k], q1r.at[stream, part, k])
        add_into(p2.at[part], (pp.at[part, m], r2.at[part, 0], r2.at[part, 1]), 4, 2 - stream)
        for k in (2, 1, 3):
            q2(stream, part, k).start()

    def q2_finish(stream, part):
        p2, r3 = streams[stream][3:]
        n = coord[part][1]
        for k in (1, 3, 2):
            o = other(n, k)
            landed(r3.at[part, o], q2s.at[stream, part, k], q2r.at[stream, part, o])
        total = p2[part, n].astype(F32)
        for k in (1, 2, 3):
            total = total + r3[part, other(n, k)].astype(F32)
        return total

    def q3(part):
        src = p3.at[part, pl.ds(pl.multiple_of((1 - y) * 32, 32), 32)]
        return remote(src, r4.at[part], q3s.at[part], q3r.at[part], y_dev)

    x_copy = remote(xo, xn, xws, xwr, y_dev)
    for part in (0, 1):
        project_near(part, other(coord[part][0], 2))
    pl.semaphore_wait(barrier, len(peers))
    x_copy.start()
    for part in (0, 1):
        q1(0, part, 0).start()
        q1(0, part, 1).start()
    for part in (0, 1):
        project_near(part, other(coord[part][0], 1))
        q1(0, part, 2).start()
    for part in (0, 1):
        project_near(part, other(coord[part][0], 3))
        q1(0, part, 3).start()
    for part in (0, 1):
        project_near(part, coord[part][0])
    sign = jnp.where(lax.broadcasted_iota(jnp.int32, (1, HD), 1) < 64, -1.0, 1.0)
    far_c, far_s = c1_ref[pl.ds(roll, 1), :], s1_ref[pl.ds(roll, 1), :]
    for k in (0, 1):
        vut[k] = jnp.transpose(vu_ref[k].astype(F32)).astype(BF16)

    def kv_copies(p):
        return [
            remote(b.at[y, p], b.at[y, p], kvs.at[i, p], kvr.at[i, p], y_dev)
            for i, b in enumerate((kb, vb))
        ]

    def prompt_block(p):
        load_prompt(p).wait()
        if p == 0:
            down_copy.wait()
        acc[...] = jnp.zeros_like(acc)
        sqacc[...] = jnp.zeros_like(sqacc)

        def step(i, carry):
            cols = pl.ds(pl.multiple_of(i * 1024, 1024), 1024)
            wide = xb[p % 2, :, cols].astype(F32)
            sq_wide = wide * wide
            part_sq = sq_wide[:, 0:128]
            for j in range(1, 8):
                part_sq = part_sq + sq_wide[:, j * 128 : (j + 1) * 128]
            sqacc[...] += part_sq
            scaled = (wide * gain_row[:, cols]).astype(BF16)
            acc[...] += dot(scaled, wd[cols, :])
            return carry

        lax.fori_loop(0, 8, step, 0)
        if p < 2:
            load_prompt(p + 2).start()
        inverse = lax.rsqrt(jnp.sum(sqacc[...], axis=1, keepdims=True) / MODEL + eps)
        latent = (acc[...] * inverse).astype(BF16)
        cosine = far_c * c0_ref[...] - far_s * s0_ref[...]
        sine = (far_s * c0_ref[...] + far_c * s0_ref[...]) * sign
        for k in (0, 1):
            mine = latent[:, k * RANK : (k + 1) * RANK]
            kb[y, p, k] = rotate(dot(mine, ku_ref[k]), cosine, sine).astype(BF16)
            vb[y, p, k] = nt_dot(vut[k], mine).astype(BF16)

    def send_kv(p):
        for c in kv_copies(p):
            c.start()

    prompt_block(0)
    slab_copy.wait()
    x_copy.wait_recv()
    sub8 = lax.broadcasted_iota(jnp.int32, (8, 128), 0)
    diagonal = lax.broadcasted_iota(jnp.int32, (128, 128), 0) == lax.broadcasted_iota(jnp.int32, (128, 128), 1)
    their_gain = gain_of(roll + 1 - 2 * y)
    squares = jnp.zeros((8, 128), F32)
    for d in range(4):
        mine = x_ref[d, :, y].reshape(128, 256).astype(F32)
        theirs = xn[d].reshape(128, 256).astype(F32)
        xns[d] = (theirs * their_gain).astype(BF16).reshape(4, 32, 256)
        total = jnp.sum(mine * mine + theirs * theirs, axis=1, keepdims=True)
        as_row = jnp.sum(jnp.where(diagonal, total, 0.0), axis=0, keepdims=True)
        squares = jnp.where(sub8 == d, as_row, squares)
    sq[0] = squares

    def square_copies(stage):
        me = (z, x)[stage]
        return [
            remote(
                sq.at[stage], sqr.at[stage, me], sqs.at[stage, k], sqrs.at[stage, me],
                (dev(other(me, k), x, y, t), dev(z, other(me, k), y, t))[stage],
            )
            for k in (1, 2, 3)
        ]

    def square_sum(stage):
        total = sq[stage]
        for k in (1, 2, 3):
            o = other((z, x)[stage], k)
            landed(sqr.at[stage, o], sqs.at[stage, 1], sqrs.at[stage, o])
            total = total + sqr[stage, o]
        return total

    for c in square_copies(0):
        c.start()
    for part in (0, 1):
        for k in (2, 1, 3, 0):
            project_pair(part, other(coord[part][0], k))
            for i in {2: (0, 1), 1: (2,), 3: (3,), 0: ()}[k]:
                q1(1, part, i).start()
    send_kv(0)
    for part in (0, 1):
        q1_forward(0, part)
    prompt_block(1)
    send_kv(1)
    for part in (0, 1):
        q1_forward(1, part)
    sq[1] = square_sum(0)
    for c in square_copies(1):
        c.start()
    prompt_block(2)
    send_kv(2)
    for part in (0, 1):
        q1_finish(0, part)
    for part in (0, 1):
        q1_finish(1, part)
    prompt_block(3)
    send_kv(3)
    for part in (0, 1):
        p3[part] = q2_finish(0, part).astype(BF16)
        q3(part).start()

    prompt = gp_ref[roll]
    length = len_ref[prompt]
    hi_c, hi_s = c1_ref[pl.ds(length >> 8, 1), :], s1_ref[pl.ds(length >> 8, 1), :]
    lo_c, lo_s = c0_ref[pl.ds(length & 255, 1), :], s0_ref[pl.ds(length & 255, 1), :]
    len_c, len_s = hi_c * lo_c - hi_s * lo_s, hi_s * lo_c + hi_c * lo_s
    row_c = len_c * ct_ref[...] - len_s * st_ref[...]
    row_s = (len_s * ct_ref[...] + len_c * st_ref[...]) * sign
    all_squares = square_sum(1)
    row_squares = jnp.sum(jnp.where(sub8 == z, all_squares, 0.0), axis=0, keepdims=True)
    lane = lax.broadcasted_iota(jnp.int32, (32, 128), 1)
    sub = lax.broadcasted_iota(jnp.int32, (32, 128), 0)
    row_squares = jnp.sum(
        jnp.where(lane == x * 32 + sub, row_squares, 0.0), axis=1, keepdims=True
    )
    inverse = lax.rsqrt(row_squares / MODEL + eps)

    def a1(part, k):
        m, n = coord[part]
        f = other(m, k)
        return remote(qq.at[part, m, n], qq.at[part, m, n], a1s.at[part, k], a1r.at[part, m], first_dev(part, f))

    def ring(buf, half, send, recv, part, f, k):
        n = coord[part][1]
        spot = buf.at[part, f, (n, n, other(n, 3), other(n, 1))[k]]
        if k >= 2:
            spot = spot.at[pl.ds((k - 2) * half, half)]
        to = second_dev(part, other(n, (1, 3)[k % 2]))
        return remote(spot, spot, send.at[part, f, k], recv.at[part, f, k], to)

    def ring_near(buf, half, send, recv, part, f):
        n = coord[part][1]
        for k in (0, 1):
            landed(buf.at[part, f, other(n, (3, 1)[k])], send.at[part, f, k], recv.at[part, f, k])
            ring(buf, half, send, recv, part, f, 2 + k).start()

    def ring_far(buf, half, send, recv, part, f):
        spot = buf.at[part, f, other(coord[part][1], 2)]
        for k in (2, 3):
            landed(spot.at[pl.ds((k - 2) * half, half)], send.at[part, f, k], recv.at[part, f, k])

    q_ring = (qq, 64, a2s, a2r)
    h_ring = (hh, 16, a2s, h2r)

    kept = []
    for part in (0, 1):
        m, n = coord[part]
        landed(r4.at[part], q3s.at[part], q3r.at[part])
        near = p3[part, pl.ds(pl.multiple_of(y * 32, 32), 32), :].astype(F32) + r4[part].astype(F32)
        near = near * inverse
        pair = q2_finish(1, part) * inverse
        heads = [rotate(near[:, h * HD : (h + 1) * HD], row_c, row_s) for h in range(8)]
        queries = jnp.transpose(jnp.concatenate(heads, axis=0)).astype(BF16)
        qq[part, m, n] = queries
        for k in (2, 1, 3):
            a1(part, k).start()
        for k in (0, 1):
            ring(*q_ring, part, m, k).start()
        kept.append((queries, pair.astype(BF16)))

    wo_copy = remote(wo_ref, wor, wos, worr, y_dev)
    wo_load.wait()
    wo_copy.start()

    key_i = lax.broadcasted_iota(jnp.int32, (32, 256), 0)
    row_i = lax.broadcasted_iota(jnp.int32, (32, 256), 1) % 32
    allowed = (key_i // STEPS == row_i // STEPS) & (key_i <= row_i)
    for part in (0, 1):
        queries, latent = kept[part]
        keys = rotate(dot(latent, ku_ref[part]), row_c, row_s).astype(BF16)
        scores = jnp.where(allowed, dot(keys, queries) * SCALE2, NEG)
        top = jnp.max(scores, axis=0, keepdims=True)
        weights = jnp.exp2(scores - top)
        values = nt_dot(vut[part], latent).astype(BF16)
        selfo[part] = dot(values, weights.astype(BF16))
        selfs[part, 0:1, :] = top
        selfs[part, 1:2, :] = jnp.sum(weights, axis=0, keepdims=True)

    for p in range(4):
        for i, b in enumerate((kb, vb)):
            landed(b.at[1 - y, p], kvs.at[i, p], kvr.at[i, p])
    base = (z * 4 + x) * (2 * TOKENS)

    token = lax.broadcasted_iota(jnp.int32, (TOKENS, HD), 0)
    first = lax.broadcasted_iota(jnp.int32, (TOKENS, HD), 1) == 0
    for p in range(4):
        for half in (0, 1):
            past = token >= len_ref[p] - base - half * TOKENS
            bias[p, half] = jnp.where(first & past, NEG, 0.0).astype(BF16)
    ones_row = jnp.where(lax.broadcasted_iota(jnp.int32, (HD, 256), 0) == 0, 1.0, 0.0).astype(BF16)
    ones_tail = jnp.ones((16, TOKENS), BF16)

    def attend(part, f, s):
        group = (f * 8 + s * 2 if part == 0 else s * 8 + f * 2) + y
        chosen = gp_ref[group]
        queries = jnp.concatenate([qq[part, f, s], ones_row], axis=0)
        scores = [
            dot(jnp.concatenate([kb[half, chosen, part], bias[chosen, half]], axis=1), queries)
            for half in (0, 1)
        ]
        top = jnp.max(jnp.maximum(scores[0], scores[1]), axis=0, keepdims=True)
        shift = top * SCALE2
        weights = [jnp.exp2(sc * SCALE2 - shift).astype(BF16) for sc in scores]
        mixed = dot(jnp.concatenate([vb[0, chosen, part], ones_tail], axis=0), weights[0])
        mixed = mixed + dot(jnp.concatenate([vb[1, chosen, part], ones_tail], axis=0), weights[1])
        store(oo.at[part, f, s], mixed[0:HD], shift, mixed[HD : HD + 1])

    def b1(part, f, s):
        n = coord[part][1]
        return remote(
            oo.at[part, f, s], orr.at[part, n, f], b1s.at[part, f, s], b1r.at[part, n, f], second_dev(part, s)
        )

    def b3(part, f):
        m = coord[part][0]
        return remote(o2.at[part, f], o2r.at[part, m], b3s.at[part, f], b3r.at[part, m], first_dev(part, f))

    for part in (0, 1):
        m, n = coord[part]
        for k in (1, 3, 2):
            f = other(m, k)
            landed(qq.at[part, f, n], a1s.at[part, k], a1r.at[part, f])
            for j in (0, 1):
                ring(*q_ring, part, f, j).start()

    def own_column(i, carry):
        for part in (0, 1):
            m, n = coord[part]
            attend(part, other(m, i), n)
        return carry

    lax.fori_loop(0, 4, own_column, 0)

    def forward(i):
        for part in (0, 1):
            ring_near(*q_ring, part, other(coord[part][0], i))

    def answer(part, i, k):
        m, n = coord[part]
        f, s = other(m, i), other(n, k)
        attend(part, f, s)
        b1(part, f, s).start()

    def near_columns(i):
        def step(j, carry):
            for part in (0, 1):
                answer(part, i, 1 + 2 * j)
            return carry

        lax.fori_loop(0, 2, step, 0)

    def far_column(i):
        for part in (0, 1):
            ring_far(*q_ring, part, other(coord[part][0], i))
            answer(part, i, 2)

    def merge_column(part, f):
        n = coord[part][1]
        found = [fetch(oo.at[part, f, n])]
        for k in (1, 3, 2):
            o = other(n, k)
            landed(orr.at[part, o, f], b1s.at[part, 0, 0], b1r.at[part, o, f])
            found.append(fetch(orr.at[part, o, f]))
        store(o2.at[part, f], *merge(*zip(*found)))

    def merge_columns(i):
        for part in (0, 1):
            f = other(coord[part][0], i)
            merge_column(part, f)
            if i:
                b3(part, f).start()

    forward(0)
    forward(1)
    near_columns(1)
    forward(2)
    far_column(1)
    near_columns(2)
    forward(3)
    far_column(2)
    near_columns(3)
    merge_columns(1)
    near_columns(0)
    far_column(3)
    merge_columns(2)
    far_column(0)
    merge_columns(3)
    merge_columns(0)

    for part in (0, 1):
        for k in (1, 2, 3):
            a1(part, k).wait_send()
        for f in range(4):
            for k in range(4):
                ring(*q_ring, part, f, k).wait_send()

    def h1(part, k):
        m, n = coord[part]
        return remote(
            hh.at[part, m, n], hh.at[part, m, n], a1s.at[part, k], h1r.at[part, m], first_dev(part, other(m, k))
        )

    for part in (0, 1):
        m, n = coord[part]
        found = [(selfo[part], selfs[part, 0:1, :], selfs[part, 1:2, :]), fetch(o2.at[part, m])]
        for k in (1, 3, 2):
            f = other(m, k)
            landed(o2r.at[part, f], b3s.at[part, 0], b3r.at[part, f])
            found.append(fetch(o2r.at[part, f]))
        mixed, _, total = merge(*zip(*found))
        heads = jnp.transpose(mixed / total).astype(BF16)
        for h in range(8):
            hh[part, m, n, :, h * HD : (h + 1) * HD] = heads[h * 32 : (h + 1) * 32, :]
        for k in (2, 1, 3):
            h1(part, k).start()
        for k in (0, 1):
            ring(*h_ring, part, m, k).start()
    for part in (0, 1):
        m, n = coord[part]
        for k in (1, 3, 2):
            f = other(m, k)
            landed(hh.at[part, f, n], a1s.at[part, k], h1r.at[part, f])
            for j in (0, 1):
                ring(*h_ring, part, f, j).start()
    for i in (0, 3, 1, 2):
        for part in (0, 1):
            ring_near(*h_ring, part, other(coord[part][0], i))
    wo_copy.wait_recv()

    def out_block(tt):
        left = hh[0, tt].reshape(128, 1024)
        right = hh[1, :, tt].reshape(128, 1024)
        for where, weight in ((y, wo_ref), (1 - y, wor)):
            got = dot(left, weight[0:1024, :]) + dot(right, weight[1024:2048, :])
            ob[tt, where] = got.astype(BF16)

    def core_copy(tt):
        return remote(ob.at[tt], obc.at[tt // 2], ocs.at[tt // 2], ocr.at[tt // 2], core_dev)

    def chip_copy(half, yy):
        return remote(
            ob2.at[half, yy], obr.at[t // 2, y], obs.at[half, yy], obrr.at[t // 2, y],
            dev(z, x, yy, half * 2 + core),
        )

    for k in (0, 3, 1, 2):
        tt = other(z, k)
        ring_far(*h_ring, 0, tt)
        if k == 2:
            for f in range(4):
                ring_far(*h_ring, 1, f)
        out_block(tt)
        half = tt // 2

        @pl.when(tt % 2 != core)
        def _():
            core_copy(tt).start()

        @pl.when(tt % 2 == core)
        def _():
            landed(obc.at[half], ocs.at[0], ocr.at[half])
            ob2[half] = (ob[tt].astype(F32) + obc[half].astype(F32)).astype(BF16)
            chip_copy(half, 1 - y).start()

            @pl.when(half != t // 2)
            def _():
                chip_copy(half, y).start()

    here = t // 2
    for yy_k in (0, 1):
        yy = y if yy_k == 0 else 1 - y
        landed(obr.at[1 - here, yy], obs.at[0, 0], obrr.at[1 - here, yy])
        total = obr[1 - here, yy].astype(F32)
        if yy_k == 0:
            total = total + ob2[here, y].astype(F32)
        else:
            landed(obr.at[here, yy], obs.at[0, 0], obrr.at[here, yy])
            total = total + obr[here, yy].astype(F32)
        out_ref[:, yy] = total.astype(BF16).reshape(4, 32, 256)

    for part in (0, 1):
        m, n = coord[part]
        for stream in (0, 1):
            for k in range(6):
                q1(stream, part, k).wait_send()
            for k in (1, 2, 3):
                q2(stream, part, k).wait_send()
        for k in (1, 2, 3):
            h1(part, k).wait_send()
            b3(part, other(m, k)).wait_send()
        q3(part).wait_send()
        for i in range(4):
            for k in (1, 2, 3):
                b1(part, other(m, i), other(n, k)).wait_send()
            for k in range(4):
                ring(*h_ring, part, i, k).wait_send()
    for stage in range(2):
        for c in square_copies(stage):
            c.wait_send()
    for p in range(4):
        for c in kv_copies(p):
            c.wait_send()
    wo_copy.wait_send()
    x_copy.wait_send()
    for half in (0, 1):
        core_copy(2 * half + 1 - core).wait_send()
        chip_copy(half, 1 - y).wait_send()
    chip_copy(1 - here, y).wait_send()


def local(
    prompt_states, decode_states, norm_gain, latent_down, key_up, value_up, query_weight, out_weight,
    prompt_lengths, group_prompt,
):
    tables = [jnp.asarray(v) for v in rope_tables()]
    vmem = pl.BlockSpec(memory_space=pltpu.VMEM)
    smem = pl.BlockSpec(memory_space=pltpu.SMEM)
    hbm = pl.BlockSpec(memory_space=pl.ANY)
    V, D = pltpu.VMEM, pltpu.SemaphoreType.DMA
    scratch = [
        V((1, MODEL), F32), V((512, 512), BF16), V((2048, 256), BF16), V((MODEL, 512), BF16), V((2, TOKENS, MODEL), BF16),
        V((TOKENS, 512), F32), V((TOKENS, 128), F32),
        V((4, 4, 2, 32, 256), BF16), V((4, 4, 32, 256), BF16), V((4, 4, 32, 256), BF16), V((4, 4, 32, 256), BF16),
        V((2, 256, NEAR), BF16),
        V((2, 4, 4, 64, NEAR), BF16), V((2, 4, 4, 32, PAIR), BF16),
        V((2, 2, 2, 64, NEAR), BF16), V((2, 2, 2, 32, PAIR), BF16),
        V((2, 2, 4, 64, NEAR), BF16), V((2, 2, 4, 32, PAIR), BF16),
        V((2, 4, 64, NEAR), BF16), V((2, 4, 32, PAIR), BF16),
        V((2, 4, 64, NEAR), BF16), V((2, 4, 32, PAIR), BF16),
        V((2, 64, NEAR), BF16), V((2, 32, NEAR), BF16),
        V((2, 8, 128), F32), V((2, 4, 8, 128), F32),
        V((2, 4, 2, TOKENS, HD), BF16), V((2, 4, 2, HD, TOKENS), BF16), V((2, HD, RANK), BF16),
        V((4, 2, TOKENS, HD), BF16),
        V((2, 4, 4, HD, 256), BF16), V((2, 4, 4, MIX, 256), BF16), V((2, 4, 4, MIX, 256), BF16),
        V((2, 4, MIX, 256), BF16), V((2, 4, MIX, 256), BF16),
        V((2, HD, 256), F32), V((2, 8, 256), F32),
        V((2, 4, 4, 32, 1024), BF16), V((2048, 256), BF16),
        V((4, 2, 128, 256), BF16), V((2, 2, 128, 256), BF16), V((2, 2, 128, 256), BF16), V((2, 2, 128, 256), BF16),
        D((7,)), D((2,)), D, D, D((2, 2, 6)), D((2, 2, 6)), D((2, 2, 4)), D((2, 2, 4)), D((2,)), D((2,)),
        D((2, 4)), D((2, 4)),
        D((2, 4)), D((2, 4)),
        D((2, 4)), D((2, 4)), D((2, 4, 4)), D((2, 4, 4)), D((2, 4, 4)), D((2, 4, 4)),
        D((2, 4)), D((2, 4)), D((2, 4)), D((2, 4, 4)), D, D,
        D((2,)), D((2,)), D((2, 2)), D((2, 2)),
    ]
    out = pl.pallas_call(
        kernel,
        out_shape=jax.ShapeDtypeStruct((4, 2, 32, 256), BF16),
        in_specs=[vmem] * 10 + [smem] * 2 + [hbm] * 4,
        out_specs=vmem,
        scratch_shapes=scratch,
        compiler_params=pltpu.CompilerParams(
            collective_id=0, has_side_effects=True, vmem_limit_bytes=60 * 1024 * 1024
        ),
        cost_estimate=pl.CostEstimate(flops=16_000_000_000, bytes_accessed=30_000_000, transcendentals=5_000_000),
        name="decode_attention",
    )(
        decode_states.reshape(4, 4, 2, 32, 256), norm_gain, key_up, value_up,
        *tables, prompt_lengths, group_prompt, query_weight, latent_down, out_weight,
        prompt_states,
    )
    return out.reshape(256, 256)


def solution(mesh):
    return jax.shard_map(
        local,
        mesh=mesh,
        in_specs=(
            P(None, "roll", None),
            P(None, "roll"),
            P(),
            P(None, "tp"),
            P("tp", None, None),
            P("tp", None, None),
            P("roll", "tp"),
            P("tp", "roll"),
            P(),
            P(),
        ),
        out_specs=P("tp", "roll"),
        check_vma=False,
    )
```

```python
import functools

import jax
import jax.numpy as jnp
import numpy as np
from jax import lax
from jax.experimental import pallas as pl
from jax.experimental.pallas import tpu as pltpu
from jax.sharding import PartitionSpec as P

HD = 128
RANK = 256
STEPS = 4
MODEL = 8192
TOKENS = 256
NEAR = 1024
PAIR = 256
MIX = HD + 16
eps = 1e-06
rope_base = 1000000.0
SCALE2 = HD ** (-0.5) * float(np.log2(np.e))
NEG = -1.0e38
F32 = jnp.float32
BF16 = jnp.bfloat16
MESH_ID = pl.DeviceIdType.MESH


def rope_tables():
    freq = rope_base ** (-(np.arange(64, dtype=np.float64) * 2.0 / HD))
    freq = np.concatenate([freq, freq])

    def pair(positions):
        angles = positions[:, None] * freq[None, :]
        return np.cos(angles).astype(np.float32), np.sin(angles).astype(np.float32)

    fine = pair(np.arange(TOKENS, dtype=np.float64))
    coarse = pair(np.arange(40, dtype=np.float64) * TOKENS)
    steps = pair(np.arange(32, dtype=np.float64) % STEPS)
    return fine + coarse + steps


def rotate(values, cosine, signed_sine):
    return values * cosine + pltpu.roll(values, 64, 1) * signed_sine


def nt_dot(a, b):
    return lax.dot_general(a, b, (((1,), (1,)), ((), ())), preferred_element_type=F32)


def dot(a, b):
    return jnp.dot(a, b, preferred_element_type=F32)


def merge(outs, maxes, sums):
    top = functools.reduce(jnp.maximum, maxes)
    factors = [jnp.exp2(m - top) for m in maxes]
    total = sum(f * s for f, s in zip(factors, sums))
    mixed = sum(f * o for f, o in zip(factors, outs))
    return mixed, top, total


def terms(value):
    high = value.astype(BF16).astype(F32)
    rest = value - high
    middle = rest.astype(BF16).astype(F32)
    return [high, middle, rest - middle]


def store(ref, mixed, top, total):
    ref[0:HD] = mixed.astype(BF16)
    row = lax.broadcasted_iota(jnp.int32, (16, top.shape[1]), 0)
    tail = jnp.zeros((16, top.shape[1]), F32)
    for i, term in enumerate(terms(top) + terms(total)):
        tail = jnp.where(row == i, term, tail)
    ref[HD:MIX] = tail.astype(BF16)


def fetch(ref):
    tail = ref[HD:MIX].astype(F32)
    top = tail[0:1] + tail[1:2] + tail[2:3]
    total = tail[3:4] + tail[4:5] + tail[5:6]
    return ref[0:HD].astype(F32), top, total


def kernel(
    x_ref, gain_ref, ku_ref, vu_ref,
    c0_ref, s0_ref, c1_ref, s1_ref, ct_ref, st_ref,
    len_ref, gp_ref, wq_hbm, down_hbm, wo_hbm, ps_hbm,
    out_ref,
    gain_row, slab, wo_ref, wd, xb, acc, sqacc, xs, xo, xn, xns, wq,
    pn, pg, r1n, r1g, r2n, r2g, p2n, p2g, r3n, r3g, p3, r4, sq, sqr,
    kb, vb, vut, bias, qq, oo, orr, o2, o2r, selfo, selfs, hh, wor, ob, obc, ob2, obr,
    loc_sem, wq_sem, xws, xwr, q1s, q1r, q2s, q2r, q3s, q3r, sqs, sqrs, kvs, kvr,
    a1s, a1r, a2s, a2r, b1s, b1r, b3s, b3r, h1r, h2r, wos, worr,
    ocs, ocr, obs, obrr,
):
    roll = lax.axis_index("roll")
    t = lax.axis_index("tp")
    z, x, y = roll // 8, (roll // 2) % 4, roll % 2
    coord = ((z, x), (x, z))

    def dev(zz, xx, yy, tt):
        return {"roll": zz * 8 + xx * 2 + yy, "tp": tt}

    def first_dev(part, f):
        return dev(f, x, y, t) if part == 0 else dev(z, f, y, t)

    def second_dev(part, s):
        return dev(z, s, y, t) if part == 0 else dev(s, x, y, t)

    y_dev = dev(z, x, 1 - y, t)
    core = t % 2
    core_dev = dev(z, x, y, t + 1 - 2 * core)

    def remote(src, dst, ss, rs, where):
        return pltpu.make_async_remote_copy(
            src_ref=src, dst_ref=dst, send_sem=ss, recv_sem=rs, device_id=where, device_id_type=MESH_ID
        )

    def landed(dst, ss, rs):
        remote(dst, dst, ss, rs, y_dev).wait_recv()

    def sent(src, ss, rs):
        remote(src, src, ss, rs, y_dev).wait_send()

    def other(i, k):
        return (i + k) % 4

    slab_copy = pltpu.make_async_copy(
        down_hbm.at[pl.ds(pl.multiple_of((roll - y) * 256, 256), 512)], slab, loc_sem.at[0]
    )
    slab_copy.start()
    wq_copies = [
        pltpu.make_async_copy(wq_hbm.at[:, i * NEAR : (i + 1) * NEAR], wq.at[i], wq_sem.at[i]) for i in range(2)
    ]
    for c in wq_copies:
        c.start()
    down_copy = pltpu.make_async_copy(down_hbm, wd, loc_sem.at[1])
    down_copy.start()

    def load_prompt(p):
        return pltpu.make_async_copy(ps_hbm.at[p], xb.at[p % 2], loc_sem.at[2 + p])

    load_prompt(0).start()
    load_prompt(1).start()
    wo_load = pltpu.make_async_copy(wo_hbm, wo_ref, loc_sem.at[6])
    wo_load.start()

    barrier = pltpu.get_barrier_semaphore()
    peers = [dev(other(z, k), x, y, t) for k in (1, 2, 3)]
    peers += [dev(z, other(x, k), y, t) for k in (1, 2, 3)]
    peers += [y_dev, core_dev, dev(z, x, y, (t + 2) % 4), dev(z, x, 1 - y, (t + 2) % 4)]
    for peer in peers:
        pl.semaphore_signal(barrier, inc=1, device_id=peer, device_id_type=MESH_ID)

    streams = ((pn, r1n, r2n, p2n, r3n), (pg, r1g, r2g, p2g, r3g))

    def gain_of(owner):
        return gain_row[:, pl.ds(pl.multiple_of(owner * 256, 256), 256)]

    for i in range(8):
        gain_row[:, i * 1024 : (i + 1) * 1024] = gain_ref[i * 1024 : (i + 1) * 1024].astype(F32).reshape(1, 1024)
    own_gain = gain_of(roll)
    xo[...] = x_ref[:, :, 1 - y]
    for c in wq_copies:
        c.wait()
    for d in range(4):
        rows = x_ref[d].reshape(256, 256).astype(F32) * own_gain
        xs[d] = rows.astype(BF16).reshape(4, 2, 32, 256)

    def project_near(part, d):
        rows = (xs[d] if part == 0 else xs[:, d]).reshape(256, 256)
        for c in range(4):
            got = dot(rows, wq[part, :, c * 256 : (c + 1) * 256])
            pn[part, d, :, :, c * 256 : (c + 1) * 256] = got.astype(BF16).reshape(4, 64, 256)

    def project_pair(part, d):
        mine = (xs[d, :, y] if part == 0 else xs[:, d, y]).reshape(128, 256)
        theirs = (xns[d] if part == 0 else xns[:, d]).reshape(128, 256)
        cols = slice(part * RANK, (part + 1) * RANK)
        got = dot(mine, slab[pl.ds(pl.multiple_of(y * 256, 256), 256), cols])
        got = got + dot(theirs, slab[pl.ds(pl.multiple_of((1 - y) * 256, 256), 256), cols])
        pg[part, d] = got.astype(BF16).reshape(4, 32, 256)

    def q1(stream, part, k):
        pp, r1, r2 = streams[stream][:3]
        m = coord[part][0]
        right, left = first_dev(part, other(m, 1)), first_dev(part, other(m, 3))
        lo, hi = pl.ds(0, 2), pl.ds(2, 2)
        far, near_r, near_l = other(m, 2), other(m, 1), other(m, 3)
        src, dst, where = (
            (pp.at[part, far, lo], r1.at[part, 0], right),
            (pp.at[part, far, hi], r1.at[part, 1], left),
            (pp.at[part, near_r, hi], r2.at[part, 0, hi], right),
            (pp.at[part, near_l, lo], r2.at[part, 1, lo], left),
            (pp.at[part, near_r, lo], r2.at[part, 0, lo], right),
            (pp.at[part, near_l, hi], r2.at[part, 1, hi], left),
        )[k]
        return remote(src, dst, q1s.at[stream, part, k], q1r.at[stream, part, k], where)

    def add_into(dst, sources, blocks, per):
        def step(i, carry):
            rows = pl.ds(pl.multiple_of((i % per) * 32, 32), 32)
            total = sources[0][i // per, rows, :].astype(F32)
            for source in sources[1:]:
                total = total + source[i // per, rows, :].astype(F32)
            dst[i // per, rows, :] = total.astype(BF16)
            return carry

        lax.fori_loop(0, per * blocks, step, 0)

    def q1_forward(stream, part):
        pp, r1 = streams[stream][:2]
        m = coord[part][0]
        for k, d, half in ((0, other(m, 1), 0), (1, other(m, 3), 2)):
            landed(r1.at[part, k], q1s.at[stream, part, k], q1r.at[stream, part, k])
            spot = pp.at[part, d, pl.ds(half, 2)]
            add_into(spot, (spot, r1.at[part, k]), 2, 2 - stream)
            q1(stream, part, 4 + k).start()

    def q2(stream, part, k):
        p2, r3 = streams[stream][3:]
        n = coord[part][1]
        s = other(n, k)
        return remote(
            p2.at[part, s], r3.at[part, n], q2s.at[stream, part, k], q2r.at[stream, part, n], second_dev(part, s)
        )

    def q1_finish(stream, part):
        pp, _, r2, p2, _ = streams[stream]
        m = coord[part][0]
        for k, d, half in ((2, 0, 2), (3, 1, 0), (4, 0, 0), (5, 1, 2)):
            landed(r2.at[part, d, pl.ds(half, 2)], q1s.at[stream, part, k], q1r.at[stream, part, k])
        add_into(p2.at[part], (pp.at[part, m], r2.at[part, 0], r2.at[part, 1]), 4, 2 - stream)
        for k in (2, 1, 3):
            q2(stream, part, k).start()

    def q2_finish(stream, part):
        p2, r3 = streams[stream][3:]
        n = coord[part][1]
        for k in (1, 3, 2):
            o = other(n, k)
            landed(r3.at[part, o], q2s.at[stream, part, k], q2r.at[stream, part, o])
        total = p2[part, n].astype(F32)
        for k in (1, 2, 3):
            total = total + r3[part, other(n, k)].astype(F32)
        return total

    def q3(part):
        src = p3.at[part, pl.ds(pl.multiple_of((1 - y) * 32, 32), 32)]
        return remote(src, r4.at[part], q3s.at[part], q3r.at[part], y_dev)

    x_copy = remote(xo, xn, xws, xwr, y_dev)
    for part in (0, 1):
        project_near(part, other(coord[part][0], 2))
    pl.semaphore_wait(barrier, len(peers))
    x_copy.start()
    for part in (0, 1):
        q1(0, part, 0).start()
        q1(0, part, 1).start()
    for part in (0, 1):
        project_near(part, other(coord[part][0], 1))
        q1(0, part, 2).start()
    for part in (0, 1):
        project_near(part, other(coord[part][0], 3))
        q1(0, part, 3).start()
    for part in (0, 1):
        project_near(part, coord[part][0])
    sign = jnp.where(lax.broadcasted_iota(jnp.int32, (1, HD), 1) < 64, -1.0, 1.0)
    far_c, far_s = c1_ref[pl.ds(roll, 1), :], s1_ref[pl.ds(roll, 1), :]
    for k in (0, 1):
        vut[k] = jnp.transpose(vu_ref[k].astype(F32)).astype(BF16)

    def kv_copies(p):
        return [
            remote(b.at[y, p], b.at[y, p], kvs.at[i, p], kvr.at[i, p], y_dev)
            for i, b in enumerate((kb, vb))
        ]

    def prompt_block(p):
        load_prompt(p).wait()
        if p == 0:
            down_copy.wait()
        acc[...] = jnp.zeros_like(acc)
        sqacc[...] = jnp.zeros_like(sqacc)

        def step(i, carry):
            cols = pl.ds(pl.multiple_of(i * 1024, 1024), 1024)
            wide = xb[p % 2, :, cols].astype(F32)
            sq_wide = wide * wide
            part_sq = sq_wide[:, 0:128]
            for j in range(1, 8):
                part_sq = part_sq + sq_wide[:, j * 128 : (j + 1) * 128]
            sqacc[...] += part_sq
            scaled = (wide * gain_row[:, cols]).astype(BF16)
            acc[...] += dot(scaled, wd[cols, :])
            return carry

        lax.fori_loop(0, 8, step, 0)
        if p < 2:
            load_prompt(p + 2).start()
        inverse = lax.rsqrt(jnp.sum(sqacc[...], axis=1, keepdims=True) / MODEL + eps)
        latent = (acc[...] * inverse).astype(BF16)
        cosine = far_c * c0_ref[...] - far_s * s0_ref[...]
        sine = (far_s * c0_ref[...] + far_c * s0_ref[...]) * sign
        for k in (0, 1):
            mine = latent[:, k * RANK : (k + 1) * RANK]
            kb[y, p, k] = rotate(dot(mine, ku_ref[k]), cosine, sine).astype(BF16)
            vb[y, p, k] = nt_dot(vut[k], mine).astype(BF16)

    def send_kv(p):
        for c in kv_copies(p):
            c.start()

    prompt_block(0)
    slab_copy.wait()
    x_copy.wait_recv()
    sub8 = lax.broadcasted_iota(jnp.int32, (8, 128), 0)
    diagonal = lax.broadcasted_iota(jnp.int32, (128, 128), 0) == lax.broadcasted_iota(jnp.int32, (128, 128), 1)
    their_gain = gain_of(roll + 1 - 2 * y)
    squares = jnp.zeros((8, 128), F32)
    for d in range(4):
        mine = x_ref[d, :, y].reshape(128, 256).astype(F32)
        theirs = xn[d].reshape(128, 256).astype(F32)
        xns[d] = (theirs * their_gain).astype(BF16).reshape(4, 32, 256)
        total = jnp.sum(mine * mine + theirs * theirs, axis=1, keepdims=True)
        as_row = jnp.sum(jnp.where(diagonal, total, 0.0), axis=0, keepdims=True)
        squares = jnp.where(sub8 == d, as_row, squares)
    sq[0] = squares

    def square_copies(stage):
        me = (z, x)[stage]
        return [
            remote(
                sq.at[stage], sqr.at[stage, me], sqs.at[stage, k], sqrs.at[stage, me],
                (dev(other(me, k), x, y, t), dev(z, other(me, k), y, t))[stage],
            )
            for k in (1, 2, 3)
        ]

    def square_sum(stage):
        total = sq[stage]
        for k in (1, 2, 3):
            o = other((z, x)[stage], k)
            landed(sqr.at[stage, o], sqs.at[stage, 1], sqrs.at[stage, o])
            total = total + sqr[stage, o]
        return total

    for c in square_copies(0):
        c.start()
    for part in (0, 1):
        for k in (2, 1, 3, 0):
            project_pair(part, other(coord[part][0], k))
            for i in {2: (0, 1), 1: (2,), 3: (3,), 0: ()}[k]:
                q1(1, part, i).start()
    send_kv(0)
    for part in (0, 1):
        q1_forward(0, part)
    prompt_block(1)
    send_kv(1)
    for part in (0, 1):
        q1_forward(1, part)
    sq[1] = square_sum(0)
    for c in square_copies(1):
        c.start()
    prompt_block(2)
    send_kv(2)
    for part in (0, 1):
        q1_finish(0, part)
    for part in (0, 1):
        q1_finish(1, part)
    prompt_block(3)
    for part in (0, 1):
        p3[part] = q2_finish(0, part).astype(BF16)
        q3(part).start()

    prompt = gp_ref[roll]
    length = len_ref[prompt]
    hi_c, hi_s = c1_ref[pl.ds(length >> 8, 1), :], s1_ref[pl.ds(length >> 8, 1), :]
    lo_c, lo_s = c0_ref[pl.ds(length & 255, 1), :], s0_ref[pl.ds(length & 255, 1), :]
    len_c, len_s = hi_c * lo_c - hi_s * lo_s, hi_s * lo_c + hi_c * lo_s
    row_c = len_c * ct_ref[...] - len_s * st_ref[...]
    row_s = (len_s * ct_ref[...] + len_c * st_ref[...]) * sign
    all_squares = square_sum(1)
    row_squares = jnp.sum(jnp.where(sub8 == z, all_squares, 0.0), axis=0, keepdims=True)
    lane = lax.broadcasted_iota(jnp.int32, (32, 128), 1)
    sub = lax.broadcasted_iota(jnp.int32, (32, 128), 0)
    row_squares = jnp.sum(
        jnp.where(lane == x * 32 + sub, row_squares, 0.0), axis=1, keepdims=True
    )
    inverse = lax.rsqrt(row_squares / MODEL + eps)

    def a1(part, k):
        m, n = coord[part]
        f = other(m, k)
        return remote(qq.at[part, m, n], qq.at[part, m, n], a1s.at[part, k], a1r.at[part, m], first_dev(part, f))

    def ring(buf, half, send, recv, part, f, k):
        n = coord[part][1]
        spot = buf.at[part, f, (n, n, other(n, 3), other(n, 1))[k]]
        if k >= 2:
            spot = spot.at[pl.ds((k - 2) * half, half)]
        to = second_dev(part, other(n, (1, 3)[k % 2]))
        return remote(spot, spot, send.at[part, f, k], recv.at[part, f, k], to)

    def ring_near(buf, half, send, recv, part, f):
        n = coord[part][1]
        for k in (0, 1):
            landed(buf.at[part, f, other(n, (3, 1)[k])], send.at[part, f, k], recv.at[part, f, k])
            ring(buf, half, send, recv, part, f, 2 + k).start()

    def ring_far(buf, half, send, recv, part, f):
        spot = buf.at[part, f, other(coord[part][1], 2)]
        for k in (2, 3):
            landed(spot.at[pl.ds((k - 2) * half, half)], send.at[part, f, k], recv.at[part, f, k])

    q_ring = (qq, 64, a2s, a2r)
    h_ring = (hh, 16, a2s, h2r)

    kept = []
    for part in (0, 1):
        m, n = coord[part]
        landed(r4.at[part], q3s.at[part], q3r.at[part])
        near = p3[part, pl.ds(pl.multiple_of(y * 32, 32), 32), :].astype(F32) + r4[part].astype(F32)
        near = near * inverse
        pair = q2_finish(1, part) * inverse
        heads = [rotate(near[:, h * HD : (h + 1) * HD], row_c, row_s) for h in range(8)]
        queries = jnp.transpose(jnp.concatenate(heads, axis=0)).astype(BF16)
        qq[part, m, n] = queries
        for k in (2, 1, 3):
            a1(part, k).start()
        for k in (0, 1):
            ring(*q_ring, part, m, k).start()
        kept.append((queries, pair.astype(BF16)))

    wo_copy = remote(wo_ref, wor, wos, worr, y_dev)
    wo_load.wait()
    send_kv(3)

    key_i = lax.broadcasted_iota(jnp.int32, (32, 256), 0)
    row_i = lax.broadcasted_iota(jnp.int32, (32, 256), 1) % 32
    allowed = (key_i // STEPS == row_i // STEPS) & (key_i <= row_i)
    for part in (0, 1):
        queries, latent = kept[part]
        keys = rotate(dot(latent, ku_ref[part]), row_c, row_s).astype(BF16)
        scores = jnp.where(allowed, dot(keys, queries) * SCALE2, NEG)
        top = jnp.max(scores, axis=0, keepdims=True)
        weights = jnp.exp2(scores - top)
        values = nt_dot(vut[part], latent).astype(BF16)
        selfo[part] = dot(values, weights.astype(BF16))
        selfs[part, 0:1, :] = top
        selfs[part, 1:2, :] = jnp.sum(weights, axis=0, keepdims=True)

    for p in range(4):
        for i, b in enumerate((kb, vb)):
            landed(b.at[1 - y, p], kvs.at[i, p], kvr.at[i, p])
    wo_copy.start()
    base = (z * 4 + x) * (2 * TOKENS)

    token = lax.broadcasted_iota(jnp.int32, (TOKENS, HD), 0)
    first = lax.broadcasted_iota(jnp.int32, (TOKENS, HD), 1) == 0
    for p in range(4):
        for half in (0, 1):
            past = token >= len_ref[p] - base - half * TOKENS
            bias[p, half] = jnp.where(first & past, NEG, 0.0).astype(BF16)
    ones_row = jnp.where(lax.broadcasted_iota(jnp.int32, (HD, 256), 0) == 0, 1.0, 0.0).astype(BF16)
    ones_tail = jnp.ones((16, TOKENS), BF16)

    def attend(part, f, s):
        group = (f * 8 + s * 2 if part == 0 else s * 8 + f * 2) + y
        chosen = gp_ref[group]
        queries = jnp.concatenate([qq[part, f, s], ones_row], axis=0)
        scores = [
            dot(jnp.concatenate([kb[half, chosen, part], bias[chosen, half]], axis=1), queries)
            for half in (0, 1)
        ]
        top = jnp.max(jnp.maximum(scores[0], scores[1]), axis=0, keepdims=True)
        shift = top * SCALE2
        weights = [jnp.exp2(sc * SCALE2 - shift).astype(BF16) for sc in scores]
        mixed = dot(jnp.concatenate([vb[0, chosen, part], ones_tail], axis=0), weights[0])
        mixed = mixed + dot(jnp.concatenate([vb[1, chosen, part], ones_tail], axis=0), weights[1])
        store(oo.at[part, f, s], mixed[0:HD], shift, mixed[HD : HD + 1])

    def b1(part, f, s):
        n = coord[part][1]
        return remote(
            oo.at[part, f, s], orr.at[part, n, f], b1s.at[part, f, s], b1r.at[part, n, f], second_dev(part, s)
        )

    def b3(part, f):
        m = coord[part][0]
        return remote(o2.at[part, f], o2r.at[part, m], b3s.at[part, f], b3r.at[part, m], first_dev(part, f))

    for part in (0, 1):
        m, n = coord[part]
        for k in (1, 3, 2):
            f = other(m, k)
            landed(qq.at[part, f, n], a1s.at[part, k], a1r.at[part, f])
            for j in (0, 1):
                ring(*q_ring, part, f, j).start()

    def own_column(i, carry):
        for part in (0, 1):
            m, n = coord[part]
            attend(part, other(m, i), n)
        return carry

    lax.fori_loop(0, 4, own_column, 0)

    def forward(i):
        for part in (0, 1):
            ring_near(*q_ring, part, other(coord[part][0], i))

    def answer(part, i, k):
        m, n = coord[part]
        f, s = other(m, i), other(n, k)
        attend(part, f, s)
        b1(part, f, s).start()

    def near_columns(i):
        def step(j, carry):
            for part in (0, 1):
                answer(part, i, 1 + 2 * j)
            return carry

        lax.fori_loop(0, 2, step, 0)

    def far_column(i):
        for part in (0, 1):
            ring_far(*q_ring, part, other(coord[part][0], i))
            answer(part, i, 2)

    def merge_column(part, f):
        n = coord[part][1]
        found = [fetch(oo.at[part, f, n])]
        for k in (1, 3, 2):
            o = other(n, k)
            landed(orr.at[part, o, f], b1s.at[part, 0, 0], b1r.at[part, o, f])
            found.append(fetch(orr.at[part, o, f]))
        store(o2.at[part, f], *merge(*zip(*found)))

    def merge_columns(i):
        for part in (0, 1):
            f = other(coord[part][0], i)
            merge_column(part, f)
            if i:
                b3(part, f).start()

    forward(0)
    forward(1)
    near_columns(1)
    forward(2)
    far_column(1)
    near_columns(2)
    forward(3)
    far_column(2)
    near_columns(3)
    merge_columns(1)
    near_columns(0)
    far_column(3)
    merge_columns(2)
    far_column(0)
    merge_columns(3)
    merge_columns(0)

    for part in (0, 1):
        for k in (1, 2, 3):
            a1(part, k).wait_send()
        for f in range(4):
            for k in range(4):
                ring(*q_ring, part, f, k).wait_send()

    def h1(part, k):
        m, n = coord[part]
        return remote(
            hh.at[part, m, n], hh.at[part, m, n], a1s.at[part, k], h1r.at[part, m], first_dev(part, other(m, k))
        )

    for part in (0, 1):
        m, n = coord[part]
        found = [(selfo[part], selfs[part, 0:1, :], selfs[part, 1:2, :]), fetch(o2.at[part, m])]
        for k in (1, 3, 2):
            f = other(m, k)
            landed(o2r.at[part, f], b3s.at[part, 0], b3r.at[part, f])
            found.append(fetch(o2r.at[part, f]))
        mixed, _, total = merge(*zip(*found))
        heads = jnp.transpose(mixed / total).astype(BF16)
        for h in range(8):
            hh[part, m, n, :, h * HD : (h + 1) * HD] = heads[h * 32 : (h + 1) * 32, :]
        for k in (2, 1, 3):
            h1(part, k).start()
        for k in (0, 1):
            ring(*h_ring, part, m, k).start()
    for part in (0, 1):
        m, n = coord[part]
        for k in (1, 3, 2):
            f = other(m, k)
            landed(hh.at[part, f, n], a1s.at[part, k], h1r.at[part, f])
            for j in (0, 1):
                ring(*h_ring, part, f, j).start()
    for i in (0, 3, 1, 2):
        for part in (0, 1):
            ring_near(*h_ring, part, other(coord[part][0], i))
    wo_copy.wait_recv()

    def out_block(tt):
        left = hh[0, tt].reshape(128, 1024)
        right = hh[1, :, tt].reshape(128, 1024)
        for where, weight in ((y, wo_ref), (1 - y, wor)):
            got = dot(left, weight[0:1024, :]) + dot(right, weight[1024:2048, :])
            ob[tt, where] = got.astype(BF16)

    def core_copy(tt):
        return remote(ob.at[tt], obc.at[tt // 2], ocs.at[tt // 2], ocr.at[tt // 2], core_dev)

    def chip_copy(half, yy):
        return remote(
            ob2.at[half, yy], obr.at[t // 2, y], obs.at[half, yy], obrr.at[t // 2, y],
            dev(z, x, yy, half * 2 + core),
        )

    for k in (0, 3, 1, 2):
        tt = other(z, k)
        ring_far(*h_ring, 0, tt)
        if k == 2:
            for f in range(4):
                ring_far(*h_ring, 1, f)
        out_block(tt)
        half = tt // 2

        @pl.when(tt % 2 != core)
        def _():
            core_copy(tt).start()

        @pl.when(tt % 2 == core)
        def _():
            landed(obc.at[half], ocs.at[0], ocr.at[half])
            ob2[half] = (ob[tt].astype(F32) + obc[half].astype(F32)).astype(BF16)
            chip_copy(half, 1 - y).start()

            @pl.when(half != t // 2)
            def _():
                chip_copy(half, y).start()

    here = t // 2
    for yy_k in (0, 1):
        yy = y if yy_k == 0 else 1 - y
        landed(obr.at[1 - here, yy], obs.at[0, 0], obrr.at[1 - here, yy])
        total = obr[1 - here, yy].astype(F32)
        if yy_k == 0:
            total = total + ob2[here, y].astype(F32)
        else:
            landed(obr.at[here, yy], obs.at[0, 0], obrr.at[here, yy])
            total = total + obr[here, yy].astype(F32)
        out_ref[:, yy] = total.astype(BF16).reshape(4, 32, 256)

    for part in (0, 1):
        m, n = coord[part]
        for stream in (0, 1):
            for k in range(6):
                q1(stream, part, k).wait_send()
            for k in (1, 2, 3):
                q2(stream, part, k).wait_send()
        for k in (1, 2, 3):
            h1(part, k).wait_send()
            b3(part, other(m, k)).wait_send()
        q3(part).wait_send()
        for i in range(4):
            for k in (1, 2, 3):
                b1(part, other(m, i), other(n, k)).wait_send()
            for k in range(4):
                ring(*h_ring, part, i, k).wait_send()
    for stage in range(2):
        for c in square_copies(stage):
            c.wait_send()
    for p in range(4):
        for c in kv_copies(p):
            c.wait_send()
    wo_copy.wait_send()
    x_copy.wait_send()
    for half in (0, 1):
        core_copy(2 * half + 1 - core).wait_send()
        chip_copy(half, 1 - y).wait_send()
    chip_copy(1 - here, y).wait_send()


def local(
    prompt_states, decode_states, norm_gain, latent_down, key_up, value_up, query_weight, out_weight,
    prompt_lengths, group_prompt,
):
    tables = [jnp.asarray(v) for v in rope_tables()]
    vmem = pl.BlockSpec(memory_space=pltpu.VMEM)
    smem = pl.BlockSpec(memory_space=pltpu.SMEM)
    hbm = pl.BlockSpec(memory_space=pl.ANY)
    V, D = pltpu.VMEM, pltpu.SemaphoreType.DMA
    scratch = [
        V((1, MODEL), F32), V((512, 512), BF16), V((2048, 256), BF16), V((MODEL, 512), BF16), V((2, TOKENS, MODEL), BF16),
        V((TOKENS, 512), F32), V((TOKENS, 128), F32),
        V((4, 4, 2, 32, 256), BF16), V((4, 4, 32, 256), BF16), V((4, 4, 32, 256), BF16), V((4, 4, 32, 256), BF16),
        V((2, 256, NEAR), BF16),
        V((2, 4, 4, 64, NEAR), BF16), V((2, 4, 4, 32, PAIR), BF16),
        V((2, 2, 2, 64, NEAR), BF16), V((2, 2, 2, 32, PAIR), BF16),
        V((2, 2, 4, 64, NEAR), BF16), V((2, 2, 4, 32, PAIR), BF16),
        V((2, 4, 64, NEAR), BF16), V((2, 4, 32, PAIR), BF16),
        V((2, 4, 64, NEAR), BF16), V((2, 4, 32, PAIR), BF16),
        V((2, 64, NEAR), BF16), V((2, 32, NEAR), BF16),
        V((2, 8, 128), F32), V((2, 4, 8, 128), F32),
        V((2, 4, 2, TOKENS, HD), BF16), V((2, 4, 2, HD, TOKENS), BF16), V((2, HD, RANK), BF16),
        V((4, 2, TOKENS, HD), BF16),
        V((2, 4, 4, HD, 256), BF16), V((2, 4, 4, MIX, 256), BF16), V((2, 4, 4, MIX, 256), BF16),
        V((2, 4, MIX, 256), BF16), V((2, 4, MIX, 256), BF16),
        V((2, HD, 256), F32), V((2, 8, 256), F32),
        V((2, 4, 4, 32, 1024), BF16), V((2048, 256), BF16),
        V((4, 2, 128, 256), BF16), V((2, 2, 128, 256), BF16), V((2, 2, 128, 256), BF16), V((2, 2, 128, 256), BF16),
        D((7,)), D((2,)), D, D, D((2, 2, 6)), D((2, 2, 6)), D((2, 2, 4)), D((2, 2, 4)), D((2,)), D((2,)),
        D((2, 4)), D((2, 4)),
        D((2, 4)), D((2, 4)),
        D((2, 4)), D((2, 4)), D((2, 4, 4)), D((2, 4, 4)), D((2, 4, 4)), D((2, 4, 4)),
        D((2, 4)), D((2, 4)), D((2, 4)), D((2, 4, 4)), D, D,
        D((2,)), D((2,)), D((2, 2)), D((2, 2)),
    ]
    out = pl.pallas_call(
        kernel,
        out_shape=jax.ShapeDtypeStruct((4, 2, 32, 256), BF16),
        in_specs=[vmem] * 10 + [smem] * 2 + [hbm] * 4,
        out_specs=vmem,
        scratch_shapes=scratch,
        compiler_params=pltpu.CompilerParams(
            collective_id=0, has_side_effects=True, vmem_limit_bytes=60 * 1024 * 1024
        ),
        cost_estimate=pl.CostEstimate(flops=16_000_000_000, bytes_accessed=30_000_000, transcendentals=5_000_000),
        name="decode_attention",
    )(
        decode_states.reshape(4, 4, 2, 32, 256), norm_gain, key_up, value_up,
        *tables, prompt_lengths, group_prompt, query_weight, latent_down, out_weight,
        prompt_states,
    )
    return out.reshape(256, 256)


def solution(mesh):
    return jax.shard_map(
        local,
        mesh=mesh,
        in_specs=(
            P(None, "roll", None),
            P(None, "roll"),
            P(),
            P(None, "tp"),
            P("tp", None, None),
            P("tp", None, None),
            P("roll", "tp"),
            P("tp", "roll"),
            P(),
            P(),
        ),
        out_specs=P("tp", "roll"),
        check_vma=False,
    )
```
